256 devices in a mesh: tmpl: 4 (over y_lo, core), row: 64 (over z, y_hi, x).
Axes of the slice: x: 4, y: 4 (y_hi: 2, y_lo: 2; y = y_hi * 2 + y_lo), z: 8, core: 2. Of those that a mesh axis runs over, the one named last changes fastest.
Arguments:
- saved_out: bfloat16 [4, 64, 512, 512], P('tmpl', None, 'row'), may hold values from -6 to 6
- sum_out: bfloat16 [4, 64, 512, 512], P('tmpl', None, 'row'), may hold values from -135 to 135
- saved_in: bfloat16 [4, 64, 512, 512], P('tmpl', None, 'row'), may hold values from -6 to 6
- sum_in: bfloat16 [4, 64, 512, 512], P('tmpl', None, 'row'), may hold values from -135 to 135
- cotangent: bfloat16 [4, 64, 512, 512], P('tmpl', None, 'row'), may hold values from -6 to 6
- w_in: bfloat16 [2, 64, 320], replicated, may hold values from -0.75 to 0.75
- w_out: bfloat16 [2, 64, 64], replicated, may hold values from -0.75 to 0.75
- norm_gain: float32 [2, 2, 64], replicated, may hold values from 0.5 to 1.5
- norm_shift: float32 [2, 2, 64], replicated, may hold values from -3 to 3
Outputs:
- grad_trunk: bfloat16 [64, 512, 512], P(None, 'row', 'tmpl')
- grad_w_in: float32 [2, 64, 320], replicated
- grad_w_out: float32 [2, 64, 64], replicated
- grad_gain: float32 [2, 2, 64], replicated
- grad_shift: float32 [2, 2, 64], replicated
The draws below stay inside these ranges and needn't reach their ends.
All inputs are finite; a program needn't handle non-finite values.
Results may differ from the reference program's by a relative error of at most 0.015.
Values may be sent and summed in bfloat16 or wider, within the bound.
A program may use at most 64 MiB of HBM per device.

```python
import math
import jax
import jax.numpy as jnp
from jax import lax

C = 64
TEMPLATES = 4
N = 512


def level_of(own_key, extent, cuts, smallest, top_value):
    level = 1.0
    for axis_at, parts in cuts:
        heights = jax.random.uniform(jax.random.fold_in(jax.random.fold_in(own_key, 6), axis_at), (parts,), jnp.float32, smallest / len(cuts), top_value / len(cuts))
        level = level * jnp.repeat(jnp.exp(heights), extent[axis_at] // parts).reshape((-1,) + (1,) * (len(extent) - 1 - axis_at))
    return level


def scatter_about(rng, dims, width, limit, cuts=(), kind=jnp.bfloat16):
    values = width * jax.random.normal(rng, dims, jnp.float32)
    if cuts:
        values = values * level_of(rng, dims, cuts, -0.22, 0.18)
    return jnp.clip(values, -limit, limit).astype(kind)


def setup_inputs(seed: int = 0) -> dict:
    keys = jax.random.split(jax.random.key(seed), 10)
    saved_out = scatter_about(keys[0], (TEMPLATES, C, N, N), 1.0, 6.0, ((0, 4), (2, 64)))
    sum_out = scatter_about(keys[1], (TEMPLATES, C, N, N), (N ** 0.5), 135.0, ((0, 4), (2, 64)))
    saved_in = scatter_about(keys[2], (TEMPLATES, C, N, N), 1.0, 6.0, ((0, 4), (2, 64)))
    sum_in = scatter_about(keys[3], (TEMPLATES, C, N, N), (N ** 0.5), 135.0, ((0, 4), (2, 64)))
    cotangent = scatter_about(keys[4], (TEMPLATES, C, N, N), 1.0, 6.0, ((0, 4), (2, 64)))
    w_in = scatter_about(keys[5], (2, C, 5 * C), C ** -0.5, 0.75)
    w_out = scatter_about(keys[6], (2, C, C), C ** -0.5, 0.75)
    norm_gain = jnp.clip(1.0 + 0.1 * jax.random.normal(keys[7], (2, 2, C), jnp.float32), 0.5, 1.5)
    norm_shift = scatter_about(keys[8], (2, 2, C), 0.5, 3.0, (), jnp.float32)
    return dict(saved_out=saved_out, sum_out=sum_out, saved_in=saved_in, sum_in=sum_in, cotangent=cotangent, w_in=w_in, w_out=w_out, norm_gain=norm_gain, norm_shift=norm_shift)


EPSILON = 1e-05

def norm_forward(values, gain_vec, shift_vec):
    average = lax.optimization_barrier(jnp.mean(values, axis=0))
    centred = values - average
    variance = lax.optimization_barrier(jnp.mean(centred * centred, axis=0))
    inv_dev = lax.rsqrt(variance + EPSILON)
    standard = centred * inv_dev
    return (standard, inv_dev, standard * gain_vec[:, None, None] + shift_vec[:, None, None])

def norm_backward(grad_in, standard, inv_dev, gain_vec):
    scaled = grad_in * gain_vec[:, None, None]
    return inv_dev * (scaled - lax.optimization_barrier(jnp.mean(scaled, axis=0)) - standard * lax.optimization_barrier(jnp.mean(scaled * standard, axis=0)))

def product(form, left, right):
    return jnp.einsum(form, left.astype(jnp.float32), right.astype(jnp.float32), precision=lax.Precision.HIGHEST)

def prepare(saved, gains, shifts, weight_in):
    standard, inv_dev, normed = norm_forward(saved.astype(jnp.float32), gains[0], shifts[0])
    normed_b = normed.astype(jnp.bfloat16)
    projected = product('cf,crn->frn', weight_in, normed_b)
    return (standard, inv_dev, normed_b, projected)

def head(saved, saved_sum, upstream, gains, shifts, weight_in, weight_out):
    channels = weight_out.shape[0]
    projected = prepare(saved, gains, shifts, weight_in)[3]
    gate_a = jax.nn.sigmoid(projected[:channels])
    pair_a = (gate_a * projected[channels:2 * channels]).astype(jnp.bfloat16)
    gate_b = jax.nn.sigmoid(projected[2 * channels:3 * channels])
    pair_b = (gate_b * projected[3 * channels:4 * channels]).astype(jnp.bfloat16)
    gate_out = jax.nn.sigmoid(projected[4 * channels:])
    sum_standard, sum_inv, normed_two = norm_forward(saved_sum.astype(jnp.float32), gains[1], shifts[1])
    normed_two_b = normed_two.astype(jnp.bfloat16)
    update = product('cd,crn->drn', weight_out, normed_two_b)
    gated_cotan = (gate_out * upstream).astype(jnp.bfloat16)
    d_gate = upstream * update
    grad_out = product('crn,drn->cd', normed_two_b, gated_cotan)
    d_normed_two = product('cd,drn->crn', weight_out, gated_cotan)
    gain_two = lax.optimization_barrier(jnp.sum(d_normed_two * sum_standard, axis=(1, 2)))
    shift_two = lax.optimization_barrier(jnp.sum(d_normed_two, axis=(1, 2)))
    d_sum = norm_backward(d_normed_two, sum_standard, sum_inv, gains[1]).astype(jnp.bfloat16)
    return (d_sum, pair_a, pair_b, d_gate, grad_out, gain_two, shift_two)

def tail(saved, gains, shifts, weight_in, d_pair_a, d_pair_b, d_gate):
    standard, inv_dev, normed_b, projected = prepare(saved, gains, shifts, weight_in)
    channels = weight_in.shape[0]
    gate_a = jax.nn.sigmoid(projected[:channels])
    value_a = projected[channels:2 * channels]
    gate_b = jax.nn.sigmoid(projected[2 * channels:3 * channels])
    value_b = projected[3 * channels:4 * channels]
    gate_out = jax.nn.sigmoid(projected[4 * channels:])
    grad_a = d_pair_a.astype(jnp.float32)
    grad_b = d_pair_b.astype(jnp.float32)
    d_projected = jnp.concatenate([grad_a * value_a * gate_a * (1.0 - gate_a), grad_a * gate_a, grad_b * value_b * gate_b * (1.0 - gate_b), grad_b * gate_b, d_gate * gate_out * (1.0 - gate_out)], axis=0).astype(jnp.bfloat16)
    grad_in = product('crn,frn->cf', normed_b, d_projected)
    d_normed = product('cf,frn->crn', weight_in, d_projected)
    gain_one = lax.optimization_barrier(jnp.sum(d_normed * standard, axis=(1, 2)))
    shift_one = lax.optimization_barrier(jnp.sum(d_normed, axis=(1, 2)))
    d_saved = norm_backward(d_normed, standard, inv_dev, gains[0])
    return (d_saved, grad_in, gain_one, shift_one)

def triangle(d_sum, pair_a, pair_b, outgoing):
    if outgoing:
        grad_a = product('hij,hjk->hik', d_sum, pair_b)
        grad_b = product('hij,hik->hjk', d_sum, pair_a)
    else:
        grad_a = product('hkj,hij->hki', pair_b, d_sum)
        grad_b = product('hki,hij->hkj', pair_a, d_sum)
    return (grad_a.astype(jnp.bfloat16), grad_b.astype(jnp.bfloat16))

def direction(saved, saved_sum, upstream, gains, shifts, weight_in, weight_out, outgoing):
    rows = saved.shape[1]
    block_rows = math.gcd(rows, 128)
    count = rows // block_rows

    def to_blocks(values):
        return values.reshape(values.shape[0], count, block_rows, values.shape[2]).transpose(1, 0, 2, 3)

    def from_blocks(values):
        return values.transpose(1, 0, 2, 3).reshape(values.shape[1], rows, values.shape[3])

    def head_block(block_item):
        return head(block_item[0], block_item[1], block_item[2], gains, shifts, weight_in, weight_out)
    heads = lax.map(head_block, (to_blocks(saved), to_blocks(saved_sum), to_blocks(upstream)))
    d_pair_a, d_pair_b = triangle(from_blocks(heads[0]), from_blocks(heads[1]), from_blocks(heads[2]), outgoing)

    def tail_block(block_item):
        return tail(block_item[0], gains, shifts, weight_in, block_item[1], block_item[2], block_item[3])
    tails = lax.map(tail_block, (to_blocks(saved), to_blocks(d_pair_a), to_blocks(d_pair_b), heads[3]))
    result = upstream + from_blocks(tails[0])
    grads = (lax.optimization_barrier(jnp.sum(tails[1], axis=0)), lax.optimization_barrier(jnp.sum(heads[4], axis=0)), jnp.stack([lax.optimization_barrier(jnp.sum(tails[2], axis=0)), lax.optimization_barrier(jnp.sum(heads[5], axis=0))]), jnp.stack([lax.optimization_barrier(jnp.sum(tails[3], axis=0)), lax.optimization_barrier(jnp.sum(heads[6], axis=0))]))
    return (result, grads)

def reference(saved_out, sum_out, saved_in, sum_in, cotangent, w_in, w_out, norm_gain, norm_shift):

    def one_template(block_item):
        upstream = block_item[4].astype(jnp.float32)
        middle, grads_in = direction(block_item[2], block_item[3], upstream, norm_gain[1], norm_shift[1], w_in[1], w_out[1], False)
        final, grads_out = direction(block_item[0], block_item[1], middle, norm_gain[0], norm_shift[0], w_in[0], w_out[0], True)
        stacked = jax.tree.map(lambda first_dir, second_dir: jnp.stack([first_dir, second_dir]), grads_out, grads_in)
        return (final, stacked)
    finals, grads = lax.map(one_template, (saved_out, sum_out, saved_in, sum_in, cotangent))
    factor = 1.0 / (TEMPLATES * N)
    grad_trunk = lax.optimization_barrier(jnp.sum(finals, axis=0)).astype(jnp.bfloat16)
    return (grad_trunk, lax.optimization_barrier(jnp.sum(grads[0], axis=0)) * factor, lax.optimization_barrier(jnp.sum(grads[1], axis=0)) * factor, lax.optimization_barrier(jnp.sum(grads[2], axis=0)) * factor, lax.optimization_barrier(jnp.sum(grads[3], axis=0)) * factor)
```

```python
import functools

import jax
import jax.numpy as jnp
from jax import lax
from jax.experimental import pallas as pl
from jax.experimental.pallas import tpu as pltpu
from jax.sharding import PartitionSpec as P

EPSILON = 1e-05
F32 = jnp.float32
BF16 = jnp.bfloat16
MESH = pl.DeviceIdType.MESH
CH = 64
RB = 8
COLS = 512
ROWS = 512
PEERS = 64
HALF = 16


def sigmoid(values):
    return 0.5 * jnp.tanh(0.5 * values) + 0.5


def product(left, right, dims=((1,), (0,))):
    return lax.dot_general(left, right, (dims, ((), ())), preferred_element_type=F32)


def kernel(
    saved_out, sum_out, saved_in, sum_in, cotangent, w_in, w_out, gain, shift,
    trunk, params,
    weights_p, weights_q, weights_u, weights_d, perm,
    normed, normed_sum, gated, proj, stat, work, upstream, d_proj, mats, partial,
    lanes_l, lanes_r,
    send_ab, recv_ab, send_d, recv_d, send_g, recv_g, send_r, recv_r,
    param, recv_one, sum_one, recv_two, recv_three,
    send_sem, recv_sem,
):
    tm = lax.axis_index("tmpl")
    me = lax.axis_index("row")
    saved = (saved_out, saved_in)
    sums = (sum_out, sum_in)

    barrier = pltpu.get_barrier_semaphore()

    def greet_row(step, carry):
        pl.semaphore_signal(
            barrier, inc=1, device_id={"tmpl": tm, "row": me ^ step}, device_id_type=MESH
        )
        return carry

    lax.fori_loop(1, PEERS, greet_row, 0)

    def greet_tmpl(step, carry):
        pl.semaphore_signal(
            barrier, inc=1,
            device_id={"tmpl": tm ^ (step // 4), "row": me ^ (step % 4)}, device_id_type=MESH,
        )
        return carry

    lax.fori_loop(4, 16, greet_tmpl, 0)

    def expand_rows(table, dest, count, width, start):
        lane = lax.broadcasted_iota(jnp.int32, (RB, width), 1)
        row = lax.broadcasted_iota(jnp.int32, (RB, width), 0)
        mask = jnp.where((lane & 7) == row, 1.0, 0.0).astype(F32)

        def body(step, carry):
            block = work[pl.ds(pl.multiple_of(8 * step, 8), 8), :width]
            parts = [block[k : k + 1, :] * mask for k in range(8)]
            at = pl.multiple_of(64 * step, 64)
            dest[pl.ds(at, 64), start : start + width] = jnp.concatenate(parts, 0).astype(BF16)
            return carry

        lax.fori_loop(0, count // 8, body, 0)

    def one_hot(rows):
        width = rows * 8
        lane = lax.broadcasted_iota(jnp.int32, (rows, width), 1)
        row = lax.broadcasted_iota(jnp.int32, (rows, width), 0)
        return jnp.where((lane >> 3) == row, 1.0, 0.0).astype(BF16)

    def build_forward(d):
        spread = one_hot(CH)
        work[0:320, :] = product(w_in[d], spread, ((0,), (0,)))
        expand_rows(None, weights_p, 320, COLS, 0)

    def build_backward(d):
        spread = one_hot(CH)
        for part in range(5):
            work[0:CH, :] = product(w_in[d, :, part * CH : (part + 1) * CH], spread)
            expand_rows(None, weights_q, CH, COLS, part * COLS)

    def build_output(d):
        spread = one_hot(CH)
        work[0:CH, :] = product(w_out[d], spread, ((0,), (0,)))
        expand_rows(None, weights_u, CH, COLS, 0)
        work[0:CH, :] = product(w_out[d], spread)
        expand_rows(None, weights_d, CH, COLS, 0)

    def statistics(x_ref, slot):
        zero = jnp.zeros((RB, COLS), F32)

        def add(step, acc):
            for k in range(4):
                acc = acc + x_ref[4 * step + k].astype(F32)
            return acc

        mean = lax.fori_loop(0, CH // 4, add, zero) * (1.0 / CH)

        def square(step, acc):
            for k in range(4):
                off = x_ref[4 * step + k].astype(F32) - mean
                acc = acc + off * off
            return acc

        inv = lax.rsqrt(lax.fori_loop(0, CH // 4, square, zero) * (1.0 / CH) + EPSILON)
        stat[slot, 0] = mean
        stat[slot, 1] = inv
        return mean, inv

    def normalise(x_ref, mean, inv, slot, dest):
        def body(step, carry):
            parts = []
            for k in range(4):
                c = 4 * step + k
                standard = (x_ref[c].astype(F32) - mean) * inv
                parts.append(standard * gain[slot, c] + shift[slot, c])
            at = pl.multiple_of(32 * step, 32)
            dest[pl.ds(at, 32), :] = jnp.concatenate(parts, 0).astype(BF16)
            return carry

        lax.fori_loop(0, CH // 4, body, 0)

    def prepare(d):
        mean, inv = statistics(saved[d], 2 * d)
        normalise(saved[d], mean, inv, 2 * d, normed.at[d])

        def project(step, carry):
            at = pl.multiple_of(step * ROWS, ROWS)
            proj[d, step] = product(weights_p[pl.ds(at, ROWS), :], normed[d])
            return carry

        lax.fori_loop(0, 5, project, 0)

        def pairs(step, carry):
            rows = pl.ds(pl.multiple_of(16 * step, 16), 16)
            chans = pl.ds(2 * step, 2)
            for k in range(2):
                gate = sigmoid(proj[d, 2 * k, rows, :])
                proj[d, 2 * k, rows, :] = gate
                pair = gate * proj[d, 2 * k + 1, rows, :]
                send_ab[d, chans, k] = pair.reshape(2, RB, COLS).astype(BF16)
            proj[d, 4, rows, :] = sigmoid(proj[d, 4, rows, :])
            return carry

        lax.fori_loop(0, CH // 2, pairs, 0)

    def head_first(d):
        mean, inv = statistics(sums[d], 2 * d + 1)
        normalise(sums[d], mean, inv, 2 * d + 1, normed_sum)

    def backward_sums(x_ref, mean, inv, slot):
        zero = jnp.zeros((RB, COLS), F32)

        def fold(v):
            return v[:, 0:128] + v[:, 128:256] + v[:, 256:384] + v[:, 384:512]

        def body(step, carry):
            one, two = carry
            for k in range(4):
                c = 4 * step + k
                dn = work[pl.ds(pl.multiple_of(8 * c, 8), 8), :]
                standard = (x_ref[c].astype(F32) - mean) * inv
                scaled = dn * gain[slot, c]
                one = one + scaled
                two = two + scaled * standard
                partial[0, c] = fold(dn * standard)
                partial[1, c] = fold(dn)
            return one, two

        one, two = lax.fori_loop(0, CH // 4, body, (zero, zero))
        return one * (1.0 / CH), two * (1.0 / CH)

    def small_sums(d, k):
        lane = lax.broadcasted_iota(jnp.int32, (CH, 128), 1)
        total = jnp.zeros((CH, 128), F32)
        for j in range(2):
            column = jnp.sum(jnp.sum(partial[j], axis=1), axis=1, keepdims=True)
            total = total + jnp.where(lane == 2 * j + k, column, 0.0)
        return total

    def store_params(d, start, value, width):
        for block in range(8):
            for lo in range(0, width, 128):
                size = min(128, width - lo)
                at = start + lo
                half, lane = at // 256, at % 256
                param[block * 2 + half, d, :, lane : lane + size] = (
                    value[block * 8 : block * 8 + 8, lo : lo + size]
                )

    def head_second(d, read_up):
        def gating(step, carry):
            rows = pl.ds(pl.multiple_of(16 * step, 16), 16)
            gated[rows, :] = (proj[d, 4, rows, :] * read_up(step)).astype(BF16)
            return carry

        lax.fori_loop(0, CH // 2, gating, 0)
        work[...] = product(weights_u[...], normed_sum[...])

        def last_block(step, carry):
            rows = pl.ds(pl.multiple_of(16 * step, 16), 16)
            gate = proj[d, 4, rows, :]
            d_gate = read_up(step) * work[rows, :]
            at = pl.ds(pl.multiple_of(4 * ROWS + 16 * step, 16), 16)
            d_proj[at, :] = (d_gate * gate * (1.0 - gate)).astype(BF16)
            return carry

        lax.fori_loop(0, CH // 2, last_block, 0)
        work[...] = product(weights_d[...], gated[...])
        slot = 2 * d + 1
        mean, inv = stat[slot, 0], stat[slot, 1]
        one, two = backward_sums(sums[d], mean, inv, slot)

        def finish(step, carry):
            for k in range(4):
                c = 4 * step + k
                dn = work[pl.ds(pl.multiple_of(8 * c, 8), 8), :]
                standard = (sums[d][c].astype(F32) - mean) * inv
                send_d[d, c] = (inv * (dn * gain[slot, c] - one - standard * two)).astype(BF16)
            return carry

        lax.fori_loop(0, CH // 4, finish, 0)

    def spread_lanes(source, dest, start):
        moved = product(perm[...], source).astype(BF16)
        for r in range(RB):
            dest[start : start + CH, r * COLS : (r + 1) * COLS] = moved[r * CH : (r + 1) * CH, :]

    def head_params(d):
        spread_lanes(normed_sum[...], lanes_l, 0)
        spread_lanes(gated[...], lanes_r, 0)
        store_params(d, 320, product(lanes_l[...], lanes_r[0:CH, :], ((1,), (1,))), CH)
        small = small_sums(d, 1)
        store_params(d, 384, small, 128)

    def tail(d, emit):
        def blocks(step, carry):
            rows = pl.ds(pl.multiple_of(16 * step, 16), 16)
            chans = pl.ds(2 * step, 2)
            for k in range(2):
                grad = recv_g[d, chans, k].astype(F32).reshape(16, COLS)
                gate = proj[d, 2 * k, rows, :]
                value = proj[d, 2 * k + 1, rows, :]
                at = pl.ds(pl.multiple_of(2 * k * ROWS + 16 * step, 16), 16)
                d_proj[at, :] = (grad * value * gate * (1.0 - gate)).astype(BF16)
                at = pl.ds(pl.multiple_of((2 * k + 1) * ROWS + 16 * step, 16), 16)
                d_proj[at, :] = (grad * gate).astype(BF16)
            return carry

        lax.fori_loop(0, CH // 2, blocks, 0)
        work[...] = product(weights_q[...], d_proj[...])
        slot = 2 * d
        mean, inv = stat[slot, 0], stat[slot, 1]
        one, two = backward_sums(saved[d], mean, inv, slot)

        def finish(step, carry):
            for k in range(4):
                c = 4 * step + k
                rows = pl.ds(pl.multiple_of(8 * c, 8), 8)
                dn = work[rows, :]
                standard = (saved[d][c].astype(F32) - mean) * inv
                emit(c, rows, inv * (dn * gain[slot, c] - one - standard * two))
            return carry

        lax.fori_loop(0, CH // 4, finish, 0)

    def tail_params(d):
        spread_lanes(normed[d], lanes_l, 0)
        for part in range(5):
            spread_lanes(d_proj[part * ROWS : (part + 1) * ROWS, :], lanes_r, part * CH)
        store_params(d, 0, product(lanes_l[...], lanes_r[...], ((1,), (1,))), 320)
        small = small_sums(d, 0)
        for block in range(8):
            param[block * 2 + 1, d, :, 128:256] += small[block * 8 : block * 8 + 8, :]

    def exchange(source, dest, sem):
        def send(step, carry):
            peer = me ^ step
            pltpu.make_async_remote_copy(
                src_ref=source.at[peer], dst_ref=dest.at[me],
                send_sem=send_sem.at[sem], recv_sem=recv_sem.at[sem],
                device_id={"tmpl": tm, "row": peer}, device_id_type=MESH,
            ).start()
            return carry

        lax.fori_loop(1, PEERS, send, 0)
        dest[me] = source[me]

    def wait_recv(dest, sem, count):
        view = dest.at[pl.ds(0, count)]
        pltpu.make_async_copy(view, view, recv_sem.at[sem]).wait()

    def wait_send(source, sem, count):
        view = source.at[pl.ds(0, count)]
        pltpu.make_async_copy(view, view, send_sem.at[sem]).wait()

    def triangle(d):
        def load(step, carry):
            rows = pl.ds(pl.multiple_of(16 * step, 16), 16)
            peers = pl.ds(2 * step, 2)
            mats[0, rows, :] = recv_ab[d, peers, 0].astype(F32).reshape(16, COLS).astype(BF16)
            mats[1, rows, :] = recv_ab[d, peers, 1].astype(F32).reshape(16, COLS).astype(BF16)
            mats[2, rows, :] = recv_d[d, peers].astype(F32).reshape(16, COLS).astype(BF16)
            return carry

        lax.fori_loop(0, PEERS // 2, load, 0)

        def store(k):
            def body(step, carry):
                rows = pl.ds(pl.multiple_of(16 * step, 16), 16)
                send_g[d, pl.ds(2 * step, 2), k] = work[rows, :].reshape(2, RB, COLS).astype(BF16)
                return carry

            lax.fori_loop(0, PEERS // 2, body, 0)

        if d == 0:
            work[...] = product(mats[2], mats[1])
            store(0)
            work[...] = product(mats[2], mats[0], ((0,), (0,)))
            store(1)
        else:
            work[...] = product(mats[1], mats[2], ((1,), (1,)))
            store(0)
            work[...] = product(mats[0], mats[2])
            store(1)

    def read_cotangent(step):
        return cotangent[pl.ds(2 * step, 2)].astype(F32).reshape(16, COLS)

    def read_upstream(step):
        return upstream[pl.ds(pl.multiple_of(16 * step, 16), 16), :]

    build_forward(1)
    prepare(1)
    pl.semaphore_wait(barrier, PEERS - 1 + 12)
    exchange(send_ab.at[1], recv_ab.at[1], 0)
    build_output(1)
    head_first(1)
    head_second(1, read_cotangent)
    exchange(send_d.at[1], recv_d.at[1], 1)

    build_forward(0)
    prepare(0)
    exchange(send_ab.at[0], recv_ab.at[0], 3)
    lane = lax.broadcasted_iota(jnp.int32, (ROWS, ROWS), 1)
    row = lax.broadcasted_iota(jnp.int32, (ROWS, ROWS), 0)
    perm[...] = jnp.where(lane == ((row & 63) << 3) + (row >> 6), 1.0, 0.0).astype(BF16)
    head_params(1)
    build_backward(1)

    wait_recv(recv_ab.at[1], 0, PEERS - 1)
    wait_recv(recv_d.at[1], 1, PEERS - 1)
    triangle(1)
    exchange(send_g.at[1], recv_g.at[1], 2)
    build_output(0)
    head_first(0)

    wait_recv(recv_g.at[1], 2, PEERS - 1)

    def keep(c, rows, value):
        upstream[rows, :] = cotangent[c].astype(F32) + value

    tail(1, keep)
    tail_params(1)
    head_second(0, read_upstream)
    exchange(send_d.at[0], recv_d.at[0], 4)
    head_params(0)
    build_backward(0)

    wait_recv(recv_ab.at[0], 3, PEERS - 1)
    wait_recv(recv_d.at[0], 4, PEERS - 1)
    triangle(0)
    exchange(send_g.at[0], recv_g.at[0], 5)
    wait_recv(recv_g.at[0], 5, PEERS - 1)

    def spread(c, rows, value):
        total = (upstream[rows, :] + value).astype(BF16)
        for t in range(4):
            send_r[t, c] = total[:, t * 128 : (t + 1) * 128]

    tail(0, spread)

    def send_trunk(step, carry):
        peer = tm ^ step
        pltpu.make_async_remote_copy(
            src_ref=send_r.at[peer], dst_ref=recv_r.at[tm],
            send_sem=send_sem.at[6], recv_sem=recv_sem.at[6],
            device_id={"tmpl": peer, "row": me}, device_id_type=MESH,
        ).start()
        return carry

    lax.fori_loop(1, 4, send_trunk, 0)
    recv_r[tm] = send_r[tm]
    tail_params(0)

    deep, flat = me // 4, me % 4

    def send_one(step, carry):
        peer = deep ^ step
        pltpu.make_async_remote_copy(
            src_ref=param.at[peer], dst_ref=recv_one.at[deep],
            send_sem=send_sem.at[7], recv_sem=recv_sem.at[7],
            device_id={"tmpl": tm, "row": peer * 4 + flat}, device_id_type=MESH,
        ).start()
        return carry

    lax.fori_loop(1, HALF, send_one, 0)
    recv_one[deep] = param[deep]
    wait_recv(recv_one, 7, HALF - 1)
    total = recv_one[0]
    for k in range(1, HALF):
        total = total + recv_one[k]
    sum_one[0] = total
    place = tm * 4 + flat

    def send_two(step, carry):
        pltpu.make_async_remote_copy(
            src_ref=sum_one.at[0], dst_ref=recv_two.at[place],
            send_sem=send_sem.at[8], recv_sem=recv_sem.at[8],
            device_id={"tmpl": tm ^ (step // 4), "row": deep * 4 + (flat ^ (step % 4))},
            device_id_type=MESH,
        ).start()
        return carry

    lax.fori_loop(1, HALF, send_two, 0)
    recv_two[place] = sum_one[0]
    wait_recv(recv_two, 8, HALF - 1)
    total = recv_two[0]
    for k in range(1, HALF):
        total = total + recv_two[k]
    sum_one[1] = total * (1.0 / 2048.0)

    def send_three(step, carry):
        pltpu.make_async_remote_copy(
            src_ref=sum_one.at[1], dst_ref=recv_three.at[deep],
            send_sem=send_sem.at[9], recv_sem=recv_sem.at[9],
            device_id={"tmpl": tm, "row": (deep ^ step) * 4 + flat}, device_id_type=MESH,
        ).start()
        return carry

    lax.fori_loop(1, HALF, send_three, 0)
    recv_three[deep] = sum_one[1]

    wait_recv(recv_r, 6, 3)

    def gather_trunk(step, carry):
        chans = pl.ds(4 * step, 4)
        value = recv_r[0, chans].astype(F32)
        for t in range(1, 4):
            value = value + recv_r[t, chans].astype(F32)
        trunk[chans] = value.astype(BF16)
        return carry

    lax.fori_loop(0, CH // 4, gather_trunk, 0)

    wait_recv(recv_three, 9, HALF - 1)
    for block in range(8):
        for half in range(2):
            for d in range(2):
                params[d, block * 8 : block * 8 + 8, half * 256 : half * 256 + 256] = (
                    recv_three[block * 2 + half, d]
                )
    for d, base in ((1, 0), (0, 3)):
        wait_send(send_ab.at[d], base, PEERS - 1)
        wait_send(send_d.at[d], base + 1, PEERS - 1)
        wait_send(send_g.at[d], base + 2, PEERS - 1)
    wait_send(send_r, 6, 3)
    wait_send(param, 7, HALF - 1)
    wait_send(recv_two, 8, HALF - 1)
    wait_send(recv_three, 9, HALF - 1)


def shards(saved_out, sum_out, saved_in, sum_in, cotangent, w_in, w_out, norm_gain, norm_shift):
    vmem = pl.BlockSpec(memory_space=pltpu.VMEM)
    smem = pl.BlockSpec(memory_space=pltpu.SMEM)
    flat = 2 * 2
    trunk, params = pl.pallas_call(
        kernel,
        out_shape=(
            jax.ShapeDtypeStruct((CH, RB, 128), BF16),
            jax.ShapeDtypeStruct((2, CH, 512), F32),
        ),
        in_specs=[vmem] * 7 + [smem] * 2,
        out_specs=(vmem, vmem),
        scratch_shapes=[
            pltpu.VMEM((5 * ROWS, COLS), BF16),
            pltpu.VMEM((ROWS, 5 * COLS), BF16),
            pltpu.VMEM((ROWS, COLS), BF16),
            pltpu.VMEM((ROWS, COLS), BF16),
            pltpu.VMEM((ROWS, ROWS), BF16),
            pltpu.VMEM((2, ROWS, COLS), BF16),
            pltpu.VMEM((ROWS, COLS), BF16),
            pltpu.VMEM((ROWS, COLS), BF16),
            pltpu.VMEM((2, 5, ROWS, COLS), F32),
            pltpu.VMEM((4, 2, RB, COLS), F32),
            pltpu.VMEM((ROWS, COLS), F32),
            pltpu.VMEM((ROWS, COLS), F32),
            pltpu.VMEM((5 * ROWS, COLS), BF16),
            pltpu.VMEM((3, ROWS, COLS), BF16),
            pltpu.VMEM((2, CH, RB, 128), F32),
            pltpu.VMEM((CH, RB * COLS), BF16),
            pltpu.VMEM((5 * CH, RB * COLS), BF16),
            pltpu.VMEM((2, PEERS, 2, RB, COLS), BF16),
            pltpu.VMEM((2, PEERS, 2, RB, COLS), BF16),
            pltpu.VMEM((2, PEERS, RB, COLS), BF16),
            pltpu.VMEM((2, PEERS, RB, COLS), BF16),
            pltpu.VMEM((2, PEERS, 2, RB, COLS), BF16),
            pltpu.VMEM((2, PEERS, 2, RB, COLS), BF16),
            pltpu.VMEM((4, CH, RB, 128), BF16),
            pltpu.VMEM((4, CH, RB, 128), BF16),
            pltpu.VMEM((HALF, 2, 8, 256), F32),
            pltpu.VMEM((HALF, 2, 8, 256), F32),
            pltpu.VMEM((2, 2, 8, 256), F32),
            pltpu.VMEM((HALF, 2, 8, 256), F32),
            pltpu.VMEM((HALF, 2, 8, 256), F32),
            pltpu.SemaphoreType.DMA((10,)),
            pltpu.SemaphoreType.DMA((10,)),
        ],
        compiler_params=pltpu.CompilerParams(
            collective_id=0, has_side_effects=True, vmem_limit_bytes=58 * 1024 * 1024
        ),
        name="triangle_backward",
    )(
        saved_out[0], sum_out[0], saved_in[0], sum_in[0], cotangent[0], w_in, w_out,
        norm_gain.reshape(flat, CH), norm_shift.reshape(flat, CH),
    )
    small = params[:, :, 384:388].transpose(0, 2, 1)
    return trunk, params[:, :, :320], params[:, :, 320:384], small[:, 0:2], small[:, 2:4]


def solution(mesh):
    whole = P("tmpl", None, "row", None)
    in_specs = (whole, whole, whole, whole, whole, P(), P(), P(), P())
    out_specs = (P(None, "row", "tmpl"), P(), P(), P(), P())
    return jax.shard_map(shards, mesh=mesh, in_specs=in_specs, out_specs=out_specs, check_vma=False)
```

```python
import functools

import jax
import jax.numpy as jnp
from jax import lax
from jax.experimental import pallas as pl
from jax.experimental.pallas import tpu as pltpu
from jax.sharding import PartitionSpec as P

EPSILON = 1e-05
F32 = jnp.float32
BF16 = jnp.bfloat16
MESH = pl.DeviceIdType.MESH
CH = 64
RB = 8
COLS = 512
ROWS = 512
PEERS = 64
HALF = 16


def sigmoid(values):
    return 0.5 * jnp.tanh(0.5 * values) + 0.5


def product(left, right, dims=((1,), (0,))):
    return lax.dot_general(left, right, (dims, ((), ())), preferred_element_type=F32)


def kernel(
    saved_out, sum_out, saved_in, sum_in, cotangent, w_in, w_out, gain, shift,
    trunk, totals,
    weights_p, weights_q, weights_u, weights_d, perm,
    normed, normed_sum, gated, proj, stat, work, update, upstream, grad_n, d_proj, mats, partial,
    lanes_n, lanes_s, lanes_r, small,
    outbox, inbox, result, send_r, recv_r, send_h, recv_h,
    param, recv_one, part_sum, recv_two,
    send_sem, recv_sem,
):
    tm = lax.axis_index("tmpl")
    me = lax.axis_index("row")
    deep, flat = me // 8, me % 8
    board, core = tm // 2, tm % 2
    saved = (saved_out, saved_in)
    sums = (sum_out, sum_in)

    barrier = pltpu.get_barrier_semaphore()

    def greet(tmpl, row):
        pl.semaphore_signal(
            barrier, inc=1, device_id={"tmpl": tmpl, "row": row}, device_id_type=MESH
        )

    def greet_row(step, carry):
        greet(tm, me ^ step)
        return carry

    lax.fori_loop(1, PEERS, greet_row, 0)

    def greet_rest(step, carry):
        greet(tm ^ 1, (deep ^ step) * 8 + flat)
        greet(tm ^ 2, deep * 8 + (flat ^ step))
        return carry

    lax.fori_loop(0, 8, greet_rest, 0)

    def rows_of(quad):
        return pl.ds(pl.multiple_of(32 * quad, 32), 32)

    def block_rows(block, quad):
        return pl.ds(pl.multiple_of(block * ROWS + 32 * quad, 32), 32)

    def to_rows(values):
        return values.astype(F32).reshape(4 * RB, COLS)

    def to_chans(values):
        return values.reshape(4, RB, COLS).astype(BF16)

    def expand_rows(table, dest, top, start):
        lane = lax.broadcasted_iota(jnp.int32, (RB, COLS), 1)
        row = lax.broadcasted_iota(jnp.int32, (RB, COLS), 0)
        mask = jnp.where((lane & 7) == row, 1.0, 0.0).astype(F32)
        work[0:CH, :] = table

        def body(step, carry):
            block = work[pl.ds(pl.multiple_of(8 * step, 8), 8), :]
            parts = [block[k : k + 1, :] * mask for k in range(8)]
            at = pl.multiple_of(top + 64 * step, 64)
            dest[pl.ds(at, 64), start : start + COLS] = jnp.concatenate(parts, 0).astype(BF16)
            return carry

        lax.fori_loop(0, CH // 8, body, 0)

    def one_hot():
        lane = lax.broadcasted_iota(jnp.int32, (CH, COLS), 1)
        row = lax.broadcasted_iota(jnp.int32, (CH, COLS), 0)
        return jnp.where((lane >> 3) == row, 1.0, 0.0).astype(BF16)

    def build_forward(d, blocks):
        spread = one_hot()
        for b in blocks:
            table = product(w_in[d, :, b * CH : (b + 1) * CH], spread, ((0,), (0,)))
            expand_rows(table, weights_p, b * ROWS, 0)

    def build_backward(d):
        spread = one_hot()
        for b in range(5):
            table = product(w_in[d, :, b * CH : (b + 1) * CH], spread)
            expand_rows(table, weights_q, 0, b * COLS)

    def build_output(d):
        spread = one_hot()
        expand_rows(product(w_out[d], spread, ((0,), (0,))), weights_u, 0, 0)
        expand_rows(product(w_out[d], spread), weights_d, 0, 0)

    def statistics(x_ref, slot):
        zero = jnp.zeros((RB, COLS), F32)

        def add(step, acc):
            for k in range(8):
                acc = acc + x_ref[8 * step + k].astype(F32)
            return acc

        mean = lax.fori_loop(0, CH // 8, add, zero) * (1.0 / CH)

        def square(step, acc):
            for k in range(8):
                off = x_ref[8 * step + k].astype(F32) - mean
                acc = acc + off * off
            return acc

        inv = lax.rsqrt(lax.fori_loop(0, CH // 8, square, zero) * (1.0 / CH) + EPSILON)
        stat[slot, 0] = mean
        stat[slot, 1] = inv
        return mean, inv

    def normalise(x_ref, mean, inv, slot, dest):
        def body(quad, carry):
            parts = []
            for k in range(4):
                c = 4 * quad + k
                standard = (x_ref[c].astype(F32) - mean) * inv
                parts.append(standard * gain[slot, c] + shift[slot, c])
            dest[rows_of(quad), :] = jnp.concatenate(parts, 0).astype(BF16)
            return carry

        lax.fori_loop(0, CH // 4, body, 0)

    def post(kind, peer):
        pltpu.make_async_remote_copy(
            src_ref=outbox.at[kind, peer], dst_ref=inbox.at[kind, me],
            send_sem=send_sem.at[kind], recv_sem=recv_sem.at[kind],
            device_id={"tmpl": tm, "row": peer}, device_id_type=MESH,
        ).start()

    def exchange(kind, fill):
        own = me // 4
        if fill is not None:
            fill(own)
        for k in range(1, 4):
            post(kind, me ^ k)

        def body(step, carry):
            quad = own ^ step
            if fill is not None:
                fill(quad)
            for k in range(4):
                post(kind, 4 * quad + k)
            return carry

        lax.fori_loop(1, PEERS // 4, body, 0)
        inbox[kind, me] = outbox[kind, me]

    def all_quads(fill):
        def body(quad, carry):
            fill(quad)
            return carry

        lax.fori_loop(0, PEERS // 4, body, 0)

    def wait_recv(dest, sem, count):
        view = dest.at[pl.ds(0, count)]
        pltpu.make_async_copy(view, view, recv_sem.at[sem]).wait()

    def wait_send(dest, sem, count):
        view = dest.at[pl.ds(0, count)]
        pltpu.make_async_copy(view, view, send_sem.at[sem]).wait()

    def arrived(kind):
        wait_recv(inbox.at[kind], kind, PEERS - 1)

    def sent(kind):
        wait_send(inbox.at[kind], kind, PEERS - 1)

    def project(d, blocks):
        for b in blocks:
            proj[d, b] = product(weights_p[b * ROWS : (b + 1) * ROWS, :], normed[d])

    def norm_input(d):
        mean, inv = statistics(saved[d], 2 * d)
        normalise(saved[d], mean, inv, 2 * d, normed.at[d])

    def pair_fill(d, k, kind):
        def fill(quad):
            rows = rows_of(quad)
            gate = sigmoid(proj[d, 2 * k, rows, :])
            proj[d, 2 * k, rows, :] = gate
            outbox[kind, pl.ds(4 * quad, 4)] = to_chans(gate * proj[d, 2 * k + 1, rows, :])

        return fill

    def out_gate(d):
        def fill(quad):
            rows = rows_of(quad)
            proj[d, 4, rows, :] = sigmoid(proj[d, 4, rows, :])

        all_quads(fill)

    def head_first(d):
        mean, inv = statistics(sums[d], 2 * d + 1)
        normalise(sums[d], mean, inv, 2 * d + 1, normed_sum)
        update[...] = product(weights_u[...], normed_sum[...])

    def backward_sums(source, x_ref, mean, inv, slot):
        keep_at = 2 * (slot % 2)

        zero = jnp.zeros((RB, COLS), F32)

        def fold(v):
            return v[:, 0:128] + v[:, 128:256] + v[:, 256:384] + v[:, 384:512]

        def body(step, carry):
            one, two = carry
            for k in range(4):
                c = 4 * step + k
                dn = source[pl.ds(pl.multiple_of(8 * c, 8), 8), :]
                standard = (x_ref[c].astype(F32) - mean) * inv
                scaled = dn * gain[slot, c]
                one = one + scaled
                two = two + scaled * standard
                partial[keep_at, c] = fold(dn * standard)
                partial[keep_at + 1, c] = fold(dn)
            return one, two

        one, two = lax.fori_loop(0, CH // 4, body, (zero, zero))
        return one * (1.0 / CH), two * (1.0 / CH)

    def small_sums(k):
        lane = lax.broadcasted_iota(jnp.int32, (CH, 128), 1)
        total = jnp.zeros((CH, 128), F32)
        for j in range(2):
            column = jnp.sum(jnp.sum(partial[2 * k + j], axis=1), axis=1, keepdims=True)
            total = total + jnp.where(lane == 2 * j + k, column, 0.0)
        return total

    def store_params(d, late, start, value, width):
        half, lane = start // 128, start % 128
        for block in range(8):
            param[d, block * 2 + half, late, :, lane : lane + width] = (
                value[block * 8 : block * 8 + 8, :]
            )

    def head_second(d, read_up):
        def gating(quad):
            rows = rows_of(quad)
            gated[rows, :] = (proj[d, 4, rows, :] * read_up(quad)).astype(BF16)

        all_quads(gating)
        work[...] = product(weights_d[...], gated[...])
        slot = 2 * d + 1
        mean, inv = stat[slot, 0], stat[slot, 1]
        one, two = backward_sums(work, sums[d], mean, inv, slot)

        def fill(quad):
            for k in range(4):
                c = 4 * quad + k
                dn = work[pl.ds(pl.multiple_of(8 * c, 8), 8), :]
                standard = (sums[d][c].astype(F32) - mean) * inv
                outbox[6 if d == 0 else 1, c] = (
                    inv * (dn * gain[slot, c] - one - standard * two)
                ).astype(BF16)

        return fill

    def gate_block(d, read_up):
        def body(quad):
            rows = rows_of(quad)
            gate = proj[d, 4, rows, :]
            d_gate = read_up(quad) * update[rows, :]
            d_proj[block_rows(4, quad), :] = (d_gate * gate * (1.0 - gate)).astype(BF16)

        all_quads(body)

    def spread_lanes(source, dest, start):
        moved = product(perm[...], source).astype(BF16)
        for r in range(RB):
            dest[start : start + CH, r * COLS : (r + 1) * COLS] = moved[r * CH : (r + 1) * CH, :]

    def head_params(d):
        spread_lanes(normed_sum[...], lanes_s, 0)
        spread_lanes(gated[...], lanes_r, 0)
        store_params(d, 0, 192, product(lanes_s[...], lanes_r[0:CH, :], ((1,), (1,))), CH)
        small[...] = small_sums(1)

    def tail_blocks(d, k):
        kind = (8 if d == 0 else 3) + k

        def body(quad):
            rows = rows_of(quad)
            grad = to_rows(inbox[kind, pl.ds(4 * quad, 4)])
            gate = proj[d, 2 * k, rows, :]
            value = proj[d, 2 * k + 1, rows, :]
            d_proj[block_rows(2 * k, quad), :] = (grad * value * gate * (1.0 - gate)).astype(BF16)
            d_proj[block_rows(2 * k + 1, quad), :] = (grad * gate).astype(BF16)

        all_quads(body)

    def tail_first(d):
        tail_blocks(d, 0)
        grad_n[...] = product(weights_q[:, 0:1024], d_proj[0:1024, :]) + product(
            weights_q[:, 2048:2560], d_proj[2048:2560, :]
        )

    def tail_second(d):
        tail_blocks(d, 1)
        grad_n[...] += product(weights_q[:, 1024:2048], d_proj[1024:2048, :])
        slot = 2 * d
        return backward_sums(grad_n, saved[d], stat[slot, 0], stat[slot, 1], slot)

    def tail_value(d, c, one, two):
        slot = 2 * d
        mean, inv = stat[slot, 0], stat[slot, 1]
        rows = pl.ds(pl.multiple_of(8 * c, 8), 8)
        standard = (saved[d][c].astype(F32) - mean) * inv
        return rows, inv * (grad_n[rows, :] * gain[slot, c] - one - standard * two)

    def early_params(d):
        spread_lanes(normed[d], lanes_n, 0)
        for at, b in enumerate((0, 1, 4)):
            spread_lanes(d_proj[b * ROWS : (b + 1) * ROWS, :], lanes_r, at * CH)
        value = product(lanes_n[...], lanes_r[0 : 3 * CH, :], ((1,), (1,)))
        store_params(d, 0, 0, value[:, 0:128], 128)
        store_params(d, 0, 128, value[:, 128:192], CH)

    def late_params(d):
        for at, b in enumerate((2, 3)):
            spread_lanes(d_proj[b * ROWS : (b + 1) * ROWS, :], lanes_r, at * CH)
        value = product(lanes_n[...], lanes_r[0 : 2 * CH, :], ((1,), (1,)))
        store_params(d, 1, 0, value, 128)
        store_params(d, 1, 128, small[...] + small_sums(0), 128)

    first = deep * 2 + core
    second = board * 8 + flat

    def to_first(d, member, source, dest, sem):
        pltpu.make_async_remote_copy(
            src_ref=source, dst_ref=dest,
            send_sem=send_sem.at[sem], recv_sem=recv_sem.at[sem],
            device_id={"tmpl": board * 2 + member % 2, "row": (member // 2) * 8 + flat},
            device_id_type=MESH,
        ).start()

    def sum_all(ref):
        total = ref[0]
        for k in range(1, HALF):
            total = total + ref[k]
        return total

    def sums_one(d):
        sem = 18 + 3 * d

        def body(step, carry):
            member = first ^ step
            to_first(d, member, param.at[d, member], recv_one.at[d, first], sem)
            return carry

        lax.fori_loop(1, HALF, body, 0)
        recv_one[d, first] = param[d, first]

    def sums_two(d):
        sem = 18 + 3 * d
        wait_recv(recv_one.at[d], sem, HALF - 1)
        part_sum[d, 0] = sum_all(recv_one.at[d])

        def body(step, carry):
            member = second ^ step
            pltpu.make_async_remote_copy(
                src_ref=part_sum.at[d, 0], dst_ref=recv_two.at[d, second],
                send_sem=send_sem.at[sem + 1], recv_sem=recv_sem.at[sem + 1],
                device_id={"tmpl": (member // 8) * 2 + core, "row": deep * 8 + member % 8},
                device_id_type=MESH,
            ).start()
            return carry

        lax.fori_loop(1, HALF, body, 0)
        recv_two[d, second] = part_sum[d, 0]

    def sums_three(d):
        sem = 18 + 3 * d
        wait_recv(recv_two.at[d], sem + 1, HALF - 1)
        part_sum[d, 1] = sum_all(recv_two.at[d]) * (1.0 / 2048.0)

        def body(step, carry):
            to_first(d, first ^ step, part_sum.at[d, 1], totals.at[d, first], sem + 2)
            return carry

        lax.fori_loop(1, HALF, body, 0)
        totals[d, first] = part_sum[d, 1]

    def load(kind, k):
        def body(quad):
            mats[k, rows_of(quad), :] = to_rows(inbox[kind, pl.ds(4 * quad, 4)]).astype(BF16)

        all_quads(body)

    def grad_fill(kind):
        def fill(quad):
            outbox[kind, pl.ds(4 * quad, 4)] = to_chans(work[rows_of(quad), :])

        return fill

    def read_cotangent(quad):
        return to_rows(cotangent[pl.ds(4 * quad, 4)])

    def read_upstream(quad):
        return upstream[rows_of(quad), :]

    build_forward(1, (2, 3))
    norm_input(1)
    project(1, (2, 3))
    pl.semaphore_wait(barrier, PEERS - 1 + 16)
    exchange(0, pair_fill(1, 1, 0))
    build_forward(1, (4,))
    build_output(1)
    project(1, (4,))
    out_gate(1)
    head_first(1)
    exchange(1, head_second(1, read_cotangent))
    build_forward(1, (0, 1))
    project(1, (0, 1))
    lane = lax.broadcasted_iota(jnp.int32, (ROWS, ROWS), 1)
    row = lax.broadcasted_iota(jnp.int32, (ROWS, ROWS), 0)
    perm[...] = jnp.where(lane == ((row & 63) << 3) + (row >> 6), 1.0, 0.0).astype(BF16)
    sent(0)
    exchange(2, pair_fill(1, 0, 2))
    gate_block(1, read_cotangent)
    head_params(1)
    build_backward(1)
    build_forward(0, (0, 1, 2, 3, 4))
    norm_input(0)

    arrived(0)
    arrived(1)
    load(0, 1)
    load(1, 2)
    work[...] = product(mats[1], mats[2], ((1,), (1,)))
    sent(1)
    exchange(3, grad_fill(3))
    project(0, (2, 3))
    arrived(2)
    load(2, 0)
    work[...] = product(mats[0], mats[2])
    sent(2)
    exchange(4, grad_fill(4))
    all_quads(pair_fill(0, 1, 5))
    project(0, (0, 1, 4))
    all_quads(pair_fill(0, 0, 7))
    out_gate(0)
    build_output(0)
    head_first(0)
    sent(3)
    exchange(5, None)

    arrived(3)
    tail_first(1)
    early_params(1)
    arrived(4)
    one, two = tail_second(1)

    def keep(quad):
        for k in range(4):
            c = 4 * quad + k
            rows, value = tail_value(1, c, one, two)
            upstream[rows, :] = cotangent[c].astype(F32) + value

    all_quads(keep)
    sent(4)
    exchange(6, head_second(0, read_upstream))
    late_params(1)
    gate_block(0, read_upstream)
    head_params(0)
    build_backward(0)
    sent(5)
    exchange(7, None)
    sums_one(1)

    arrived(5)
    arrived(6)
    load(5, 1)
    load(6, 2)
    work[...] = product(mats[2], mats[1])
    sent(6)
    exchange(8, grad_fill(8))
    arrived(7)
    load(7, 0)
    work[...] = product(mats[2], mats[0], ((0,), (0,)))
    sent(7)
    exchange(9, grad_fill(9))
    sums_two(1)
    arrived(8)
    tail_first(0)
    early_params(0)
    sums_three(1)
    arrived(9)
    one, two = tail_second(0)
    late_params(0)
    sums_one(0)

    for part in range(4):
        def spread(step, carry):
            for k in range(4):
                c = part * 16 + 4 * step + k
                rows, value = tail_value(0, c, one, two)
                value = upstream[rows, :] + value
                for t in range(4):
                    block = value[:, t * 128 : (t + 1) * 128]
                    result[t, c] = block
                    send_r[t, c] = block.astype(BF16)
            return carry

        lax.fori_loop(0, 4, spread, 0)
        chans = pl.ds(part * 16, 16)
        for hi in range(2):
            pltpu.make_async_remote_copy(
                src_ref=send_r.at[2 * hi + (1 - core), chans], dst_ref=recv_r.at[part, hi],
                send_sem=send_sem.at[10 + part], recv_sem=recv_sem.at[10 + part],
                device_id={"tmpl": board * 2 + (1 - core), "row": me}, device_id_type=MESH,
            ).start()
    sums_two(0)
    for part in range(4):
        chans = pl.ds(part * 16, 16)
        wait_recv(recv_r.at[part], 10 + part, 2)
        total = result[2 * (1 - board) + core, chans] + recv_r[part, 1 - board].astype(F32)
        send_h[part] = total.astype(BF16)
        pltpu.make_async_remote_copy(
            src_ref=send_h.at[part], dst_ref=recv_h.at[part],
            send_sem=send_sem.at[14 + part], recv_sem=recv_sem.at[14 + part],
            device_id={"tmpl": (1 - board) * 2 + core, "row": me}, device_id_type=MESH,
        ).start()
    sums_three(0)
    for part in range(4):
        chans = pl.ds(part * 16, 16)
        view = recv_h.at[part]
        pltpu.make_async_copy(view, view, recv_sem.at[14 + part]).wait()
        total = result[tm, chans] + recv_r[part, board].astype(F32) + recv_h[part].astype(F32)
        trunk[chans] = total.astype(BF16)
    for d in range(2):
        wait_recv(totals.at[d], 20 + 3 * d, HALF - 1)
    for kind in (8, 9):
        sent(kind)
    for part in range(4):
        wait_send(recv_r.at[part], 10 + part, 2)
        view = recv_h.at[part]
        pltpu.make_async_copy(view, view, send_sem.at[14 + part]).wait()
    for d in range(2):
        wait_send(recv_one.at[d], 18 + 3 * d, HALF - 1)
        wait_send(recv_two.at[d], 19 + 3 * d, HALF - 1)
        wait_send(totals.at[d], 20 + 3 * d, HALF - 1)


def unpack(trunk, totals, out, grad_in, grad_out, grad_gain, grad_shift):
    out[...] = trunk[...]
    for d in range(2):
        for block in range(8):
            rows = slice(block * 8, block * 8 + 8)
            left, right = totals[d, 2 * block], totals[d, 2 * block + 1]
            grad_in[d, rows, 0:128] = left[0]
            grad_in[d, rows, 128:256] = left[1]
            grad_in[d, rows, 256:320] = right[0, :, 0:64]
            grad_out[d, rows, :] = right[0, :, 64:128]
        small = [totals[d, 2 * block + 1, 1] for block in range(8)]
        small = jnp.concatenate(small + [jnp.zeros((CH, 128), F32)], 0).T
        grad_gain[d] = small[0:2, 0:CH]
        grad_shift[d] = small[2:4, 0:CH]


def shards(saved_out, sum_out, saved_in, sum_in, cotangent, w_in, w_out, norm_gain, norm_shift):
    vmem = pl.BlockSpec(memory_space=pltpu.VMEM)
    smem = pl.BlockSpec(memory_space=pltpu.SMEM)
    shape = jax.ShapeDtypeStruct
    full = (ROWS, COLS)
    boxes = (10, PEERS, RB, COLS)
    trunk, totals = pl.pallas_call(
        kernel,
        out_shape=(shape((CH, RB, 128), BF16), shape((2, HALF, 2, 8, 128), F32)),
        in_specs=[vmem] * 7 + [smem] * 2,
        out_specs=(vmem, vmem),
        scratch_shapes=[
            pltpu.VMEM((5 * ROWS, COLS), BF16),
            pltpu.VMEM((ROWS, 5 * COLS), BF16),
            pltpu.VMEM(full, BF16),
            pltpu.VMEM(full, BF16),
            pltpu.VMEM(full, BF16),
            pltpu.VMEM((2, ROWS, COLS), BF16),
            pltpu.VMEM(full, BF16),
            pltpu.VMEM(full, BF16),
            pltpu.VMEM((2, 5, ROWS, COLS), F32),
            pltpu.VMEM((4, 2, RB, COLS), F32),
            pltpu.VMEM(full, F32),
            pltpu.VMEM(full, F32),
            pltpu.VMEM(full, F32),
            pltpu.VMEM(full, F32),
            pltpu.VMEM((5 * ROWS, COLS), BF16),
            pltpu.VMEM((3, ROWS, COLS), BF16),
            pltpu.VMEM((4, CH, RB, 128), F32),
            pltpu.VMEM((CH, RB * COLS), BF16),
            pltpu.VMEM((CH, RB * COLS), BF16),
            pltpu.VMEM((3 * CH, RB * COLS), BF16),
            pltpu.VMEM((CH, 128), F32),
            pltpu.VMEM(boxes, BF16),
            pltpu.VMEM(boxes, BF16),
            pltpu.VMEM((4, CH, RB, 128), F32),
            pltpu.VMEM((4, CH, RB, 128), BF16),
            pltpu.VMEM((4, 2, 16, RB, 128), BF16),
            pltpu.VMEM((4, 16, RB, 128), BF16),
            pltpu.VMEM((4, 16, RB, 128), BF16),
            pltpu.VMEM((2, HALF, 2, 8, 128), F32),
            pltpu.VMEM((2, HALF, 2, 8, 128), F32),
            pltpu.VMEM((2, 2, 2, 8, 128), F32),
            pltpu.VMEM((2, HALF, 2, 8, 128), F32),
            pltpu.SemaphoreType.DMA((24,)),
            pltpu.SemaphoreType.DMA((24,)),
        ],
        compiler_params=pltpu.CompilerParams(
            collective_id=0, has_side_effects=True, vmem_limit_bytes=58 * 1024 * 1024
        ),
        name="triangle_backward",
    )(
        saved_out[0], sum_out[0], saved_in[0], sum_in[0], cotangent[0], w_in, w_out,
        norm_gain.reshape(4, CH), norm_shift.reshape(4, CH),
    )
    return pl.pallas_call(
        unpack,
        out_shape=(
            shape((CH, RB, 128), BF16), shape((2, CH, 5 * CH), F32), shape((2, CH, CH), F32),
            shape((2, 2, CH), F32), shape((2, 2, CH), F32),
        ),
        in_specs=[vmem] * 2,
        out_specs=(vmem,) * 5,
        name="unpack",
    )(trunk, totals)


def solution(mesh):
    whole = P("tmpl", None, "row", None)
    in_specs = (whole, whole, whole, whole, whole, P(), P(), P(), P())
    out_specs = (P(None, "row", "tmpl"), P(), P(), P(), P())
    return jax.shard_map(shards, mesh=mesh, in_specs=in_specs, out_specs=out_specs, check_vma=False)
```

```python
import functools

import jax
import jax.numpy as jnp
from jax import lax
from jax.experimental import pallas as pl
from jax.experimental.pallas import tpu as pltpu
from jax.sharding import PartitionSpec as P

EPSILON = 1e-05
F32 = jnp.float32
BF16 = jnp.bfloat16
MESH = pl.DeviceIdType.MESH
CH = 64
RB = 8
COLS = 512
ROWS = 512
PEERS = 64
HALF = 16


def sigmoid(values):
    return 0.5 * jnp.tanh(0.5 * values) + 0.5


def product(left, right, dims=((1,), (0,))):
    return lax.dot_general(left, right, (dims, ((), ())), preferred_element_type=F32)


def kernel(
    saved_out, sum_out, saved_in, sum_in, cotangent, w_in, w_out, gain, shift,
    trunk, totals,
    weights_p, weights_q, weights_u, weights_d, perm,
    normed, normed_sum, gated, proj, stat, work, update, upstream, grad_n, d_proj, mats, partial,
    lanes_n, lanes_s, lanes_r, small,
    outbox, inbox, result, send_r, recv_r, send_h, recv_h,
    param, recv_one, part_sum, recv_two,
    send_sem, recv_sem,
):
    tm = lax.axis_index("tmpl")
    me = lax.axis_index("row")
    deep, flat = me // 8, me % 8
    board, core = tm // 2, tm % 2
    saved = (saved_out, saved_in)
    sums = (sum_out, sum_in)

    barrier = pltpu.get_barrier_semaphore()

    def greet(tmpl, row):
        pl.semaphore_signal(
            barrier, inc=1, device_id={"tmpl": tmpl, "row": row}, device_id_type=MESH
        )

    def greet_row(step, carry):
        greet(tm, me ^ step)
        return carry

    lax.fori_loop(1, PEERS, greet_row, 0)

    def greet_rest(step, carry):
        greet(tm ^ 1, (deep ^ step) * 8 + flat)
        greet(tm ^ 2, deep * 8 + (flat ^ step))
        return carry

    lax.fori_loop(0, 8, greet_rest, 0)

    def rows_of(quad):
        return pl.ds(pl.multiple_of(32 * quad, 32), 32)

    def block_rows(block, quad):
        return pl.ds(pl.multiple_of(block * ROWS + 32 * quad, 32), 32)

    def to_rows(values):
        return values.astype(F32).reshape(4 * RB, COLS)

    def to_chans(values):
        return values.reshape(4, RB, COLS).astype(BF16)

    def halves(step):
        return pl.ds(pl.multiple_of((step % 2) * 256, 256), 256)

    def multiply(dest, left, right, flip=False):
        def body(step, carry):
            if flip:
                dest[:, halves(step)] = product(left[...], right[halves(step), :], ((1,), (1,)))
            else:
                dest[:, halves(step)] = product(left[...], right[:, halves(step)])
            return carry

        lax.fori_loop(0, 2, body, 0)

    def expand_rows(dest, top, count):
        lane = lax.broadcasted_iota(jnp.int32, (RB, COLS), 1)
        row = lax.broadcasted_iota(jnp.int32, (RB, COLS), 0)
        mask = jnp.where((lane & 7) == row, 1.0, 0.0).astype(F32)

        def body(step, carry):
            block = work[pl.ds(pl.multiple_of(8 * step, 8), 8), :]
            parts = [block[k : k + 1, :] * mask for k in range(8)]
            at = pl.multiple_of(top + 64 * step, 64)
            dest[pl.ds(at, 64), :] = jnp.concatenate(parts, 0).astype(BF16)
            return carry

        lax.fori_loop(0, count * CH // 8, body, 0)

    def one_hot():
        lane = lax.broadcasted_iota(jnp.int32, (CH, COLS), 1)
        row = lax.broadcasted_iota(jnp.int32, (CH, COLS), 0)
        return jnp.where((lane >> 3) == row, 1.0, 0.0).astype(BF16)

    def build_forward(d, low, count):
        spread = one_hot()
        for b in range(low, low + count):
            table = product(w_in[d, :, b * CH : (b + 1) * CH], spread, ((0,), (0,)))
            work[(b - low) * CH : (b - low + 1) * CH, :] = table
        expand_rows(weights_p, low * ROWS, count)

    def build_backward(d):
        spread = one_hot()
        for b in range(5):
            table = product(w_in[d, :, b * CH : (b + 1) * CH], spread)
            work[b * CH : (b + 1) * CH, :] = table
        expand_rows(weights_q, d * 5 * ROWS, 5)

    def build_output(d):
        spread = one_hot()
        work[0:CH, :] = product(w_out[d], spread, ((0,), (0,)))
        expand_rows(weights_u, 0, 1)
        work[0:CH, :] = product(w_out[d], spread)
        expand_rows(weights_d, 0, 1)

    def statistics(x_ref, slot):
        zero = jnp.zeros((RB, COLS), F32)

        def add(step, acc):
            for k in range(8):
                acc = acc + x_ref[8 * step + k].astype(F32)
            return acc

        mean = lax.fori_loop(0, CH // 8, add, zero) * (1.0 / CH)

        def square(step, acc):
            for k in range(8):
                off = x_ref[8 * step + k].astype(F32) - mean
                acc = acc + off * off
            return acc

        inv = lax.rsqrt(lax.fori_loop(0, CH // 8, square, zero) * (1.0 / CH) + EPSILON)
        stat[slot, 0] = mean
        stat[slot, 1] = inv
        return mean, inv

    def normalise(x_ref, mean, inv, slot, dest):
        def body(quad, carry):
            parts = []
            for k in range(4):
                c = 4 * quad + k
                standard = (x_ref[c].astype(F32) - mean) * inv
                parts.append(standard * gain[slot, c] + shift[slot, c])
            dest[rows_of(quad), :] = jnp.concatenate(parts, 0).astype(BF16)
            return carry

        lax.fori_loop(0, CH // 4, body, 0)

    def post(kind, peer):
        pltpu.make_async_remote_copy(
            src_ref=outbox.at[kind, peer], dst_ref=inbox.at[kind, me],
            send_sem=send_sem.at[kind], recv_sem=recv_sem.at[kind],
            device_id={"tmpl": tm, "row": peer}, device_id_type=MESH,
        ).start()

    def exchange(kind, fill):
        own = me // 4
        if fill is not None:
            fill(own)
        for k in range(1, 4):
            post(kind, me ^ k)

        def body(step, carry):
            quad = own ^ step
            if fill is not None:
                fill(quad)
            for k in range(4):
                post(kind, 4 * quad + k)
            return carry

        lax.fori_loop(1, PEERS // 4, body, 0)
        inbox[kind, me] = outbox[kind, me]

    def all_quads(fill):
        def body(quad, carry):
            fill(quad)
            return carry

        lax.fori_loop(0, PEERS // 4, body, 0)

    def wait_recv(dest, sem, count):
        view = dest.at[pl.ds(0, count)]
        pltpu.make_async_copy(view, view, recv_sem.at[sem]).wait()

    def wait_send(dest, sem, count):
        view = dest.at[pl.ds(0, count)]
        pltpu.make_async_copy(view, view, send_sem.at[sem]).wait()

    def arrived(kind):
        wait_recv(inbox.at[kind], kind, PEERS - 1)

    def sent(kind):
        wait_send(inbox.at[kind], kind, PEERS - 1)

    def project(d, low, count):
        def body(step, carry):
            block = low + step // 2
            left = weights_p[pl.ds(pl.multiple_of(block * ROWS, ROWS), ROWS), :]
            proj[d, block, :, halves(step)] = product(left, normed[d, :, halves(step)])
            return carry

        lax.fori_loop(0, 2 * count, body, 0)

    def norm_input(d):
        mean, inv = statistics(saved[d], 2 * d)
        normalise(saved[d], mean, inv, 2 * d, normed.at[d])

    def pair_fill(d, k, kind):
        def fill(quad):
            rows = rows_of(quad)
            gate = sigmoid(proj[d, 2 * k, rows, :])
            proj[d, 2 * k, rows, :] = gate
            outbox[kind, pl.ds(4 * quad, 4)] = to_chans(gate * proj[d, 2 * k + 1, rows, :])

        return fill

    def out_gate(d):
        def fill(quad):
            rows = rows_of(quad)
            proj[d, 4, rows, :] = sigmoid(proj[d, 4, rows, :])

        all_quads(fill)

    def head_first(d):
        mean, inv = statistics(sums[d], 2 * d + 1)
        normalise(sums[d], mean, inv, 2 * d + 1, normed_sum)
        multiply(update, weights_u, normed_sum)

    def backward_sums(source, x_ref, mean, inv, slot):
        keep_at = 2 * (slot % 2)

        zero = jnp.zeros((RB, COLS), F32)

        def fold(v):
            return v[:, 0:128] + v[:, 128:256] + v[:, 256:384] + v[:, 384:512]

        def body(step, carry):
            one, two = carry
            for k in range(4):
                c = 4 * step + k
                dn = source[pl.ds(pl.multiple_of(8 * c, 8), 8), :]
                standard = (x_ref[c].astype(F32) - mean) * inv
                scaled = dn * gain[slot, c]
                one = one + scaled
                two = two + scaled * standard
                partial[keep_at, c] = fold(dn * standard)
                partial[keep_at + 1, c] = fold(dn)
            return one, two

        one, two = lax.fori_loop(0, CH // 4, body, (zero, zero))
        return one * (1.0 / CH), two * (1.0 / CH)

    def small_sums(k):
        lane = lax.broadcasted_iota(jnp.int32, (CH, 128), 1)
        total = jnp.zeros((CH, 128), F32)
        for j in range(2):
            column = jnp.sum(jnp.sum(partial[2 * k + j], axis=1), axis=1, keepdims=True)
            total = total + jnp.where(lane == 2 * j + k, column, 0.0)
        return total

    def store_params(d, late, start, value, width):
        half, lane = start // 128, start % 128
        for block in range(8):
            param[d, block * 2 + half, late, :, lane : lane + width] = (
                value[block * 8 : block * 8 + 8, :]
            )

    def head_second(d, read_up):
        def gating(quad):
            rows = rows_of(quad)
            gated[rows, :] = (proj[d, 4, rows, :] * read_up(quad)).astype(BF16)

        all_quads(gating)
        multiply(work, weights_d, gated)
        slot = 2 * d + 1
        mean, inv = stat[slot, 0], stat[slot, 1]
        one, two = backward_sums(work, sums[d], mean, inv, slot)

        def fill(quad):
            for k in range(4):
                c = 4 * quad + k
                dn = work[pl.ds(pl.multiple_of(8 * c, 8), 8), :]
                standard = (sums[d][c].astype(F32) - mean) * inv
                outbox[6 if d == 0 else 1, c] = (
                    inv * (dn * gain[slot, c] - one - standard * two)
                ).astype(BF16)

        return fill

    def gate_block(d, read_up):
        def body(quad):
            rows = rows_of(quad)
            gate = proj[d, 4, rows, :]
            d_gate = read_up(quad) * update[rows, :]
            d_proj[block_rows(4, quad), :] = (d_gate * gate * (1.0 - gate)).astype(BF16)

        all_quads(body)

    def spread_lanes(source, dest, count, place):
        def body(step, carry):
            at = place(step // 2)
            moved = product(perm[...], source[pl.ds(at, ROWS), halves(step)]).astype(BF16)
            rows = pl.ds(pl.multiple_of((step // 2) * CH, CH), CH)
            for r in range(RB):
                lanes = pl.ds(pl.multiple_of(r * COLS + (step % 2) * 256, 256), 256)
                dest[rows, lanes] = moved[r * CH : (r + 1) * CH, :]
            return carry

        lax.fori_loop(0, 2 * count, body, 0)

    def gram(left, count):
        def body(step, total):
            lanes = pl.ds(pl.multiple_of(step * COLS, COLS), COLS)
            return total + product(left[:, lanes], lanes_r[0 : count * CH, lanes], ((1,), (1,)))

        return lax.fori_loop(0, RB, body, jnp.zeros((CH, count * CH), F32))

    def whole(step):
        return 0

    def head_params(d):
        spread_lanes(normed_sum, lanes_s, 1, whole)
        spread_lanes(gated, lanes_r, 1, whole)
        store_params(d, 0, 192, gram(lanes_s, 1), CH)
        small[...] = small_sums(1)

    def tail_blocks(d, k):
        kind = (8 if d == 0 else 3) + k

        def body(quad):
            rows = rows_of(quad)
            grad = to_rows(inbox[kind, pl.ds(4 * quad, 4)])
            gate = proj[d, 2 * k, rows, :]
            value = proj[d, 2 * k + 1, rows, :]
            d_proj[block_rows(2 * k, quad), :] = (grad * value * gate * (1.0 - gate)).astype(BF16)
            d_proj[block_rows(2 * k + 1, quad), :] = (grad * gate).astype(BF16)

        all_quads(body)

    def add_blocks(d, count, place, fresh):
        def body(step, carry):
            at = place(step // 2)
            rows = pl.ds(at, ROWS)
            left = weights_q[pl.ds(d * 5 * ROWS + at, ROWS), :]
            value = product(left, d_proj[rows, halves(step)])
            grad_n[:, halves(step)] += value
            return carry

        if fresh:
            grad_n[...] = jnp.zeros((ROWS, COLS), F32)
        lax.fori_loop(0, 2 * count, body, 0)

    def early_place(step):
        return pl.multiple_of((step + 2 * (step // 2)) * ROWS, ROWS)

    def late_place(step):
        return pl.multiple_of((step + 2) * ROWS, ROWS)

    def tail_first(d):
        tail_blocks(d, 0)
        add_blocks(d, 3, early_place, True)

    def tail_second(d):
        tail_blocks(d, 1)
        add_blocks(d, 2, late_place, False)
        slot = 2 * d
        return backward_sums(grad_n, saved[d], stat[slot, 0], stat[slot, 1], slot)

    def tail_value(d, c, one, two):
        slot = 2 * d
        mean, inv = stat[slot, 0], stat[slot, 1]
        rows = pl.ds(pl.multiple_of(8 * c, 8), 8)
        standard = (saved[d][c].astype(F32) - mean) * inv
        return rows, inv * (grad_n[rows, :] * gain[slot, c] - one - standard * two)

    def early_params(d):
        spread_lanes(normed.at[d], lanes_n, 1, whole)
        spread_lanes(d_proj, lanes_r, 3, early_place)
        value = gram(lanes_n, 3)
        store_params(d, 0, 0, value[:, 0:128], 128)
        store_params(d, 0, 128, value[:, 128:192], CH)

    def late_params(d):
        spread_lanes(d_proj, lanes_r, 2, late_place)
        store_params(d, 1, 0, gram(lanes_n, 2), 128)
        store_params(d, 1, 128, small[...] + small_sums(0), 128)

    first = deep * 2 + core
    second = board * 8 + flat

    def to_first(d, member, source, dest, sem):
        pltpu.make_async_remote_copy(
            src_ref=source, dst_ref=dest,
            send_sem=send_sem.at[sem], recv_sem=recv_sem.at[sem],
            device_id={"tmpl": board * 2 + member % 2, "row": (member // 2) * 8 + flat},
            device_id_type=MESH,
        ).start()

    def sum_all(ref):
        total = ref[0]
        for k in range(1, HALF):
            total = total + ref[k]
        return total

    def sums_one(d):
        sem = 18 + 3 * d

        def body(step, carry):
            member = first ^ step
            to_first(d, member, param.at[d, member], recv_one.at[d, first], sem)
            return carry

        lax.fori_loop(1, HALF, body, 0)
        recv_one[d, first] = param[d, first]

    def sums_two(d):
        sem = 18 + 3 * d
        wait_recv(recv_one.at[d], sem, HALF - 1)
        part_sum[d, 0] = sum_all(recv_one.at[d])

        def body(step, carry):
            member = second ^ step
            pltpu.make_async_remote_copy(
                src_ref=part_sum.at[d, 0], dst_ref=recv_two.at[d, second],
                send_sem=send_sem.at[sem + 1], recv_sem=recv_sem.at[sem + 1],
                device_id={"tmpl": (member // 8) * 2 + core, "row": deep * 8 + member % 8},
                device_id_type=MESH,
            ).start()
            return carry

        lax.fori_loop(1, HALF, body, 0)
        recv_two[d, second] = part_sum[d, 0]

    def sums_three(d):
        sem = 18 + 3 * d
        wait_recv(recv_two.at[d], sem + 1, HALF - 1)
        part_sum[d, 1] = sum_all(recv_two.at[d]) * (1.0 / 2048.0)

        def body(step, carry):
            to_first(d, first ^ step, part_sum.at[d, 1], totals.at[d, first], sem + 2)
            return carry

        lax.fori_loop(1, HALF, body, 0)
        totals[d, first] = part_sum[d, 1]

    def load(kind, k):
        def body(quad):
            mats[k, rows_of(quad), :] = to_rows(inbox[kind, pl.ds(4 * quad, 4)]).astype(BF16)

        all_quads(body)

    def grad_fill(kind):
        def fill(quad):
            outbox[kind, pl.ds(4 * quad, 4)] = to_chans(work[rows_of(quad), :])

        return fill

    def read_cotangent(quad):
        return to_rows(cotangent[pl.ds(4 * quad, 4)])

    def read_upstream(quad):
        return upstream[rows_of(quad), :]

    build_forward(1, 2, 2)
    norm_input(1)
    project(1, 2, 2)
    pl.semaphore_wait(barrier, PEERS - 1 + 16)
    exchange(0, pair_fill(1, 1, 0))
    build_forward(1, 4, 1)
    build_output(1)
    project(1, 4, 1)
    out_gate(1)
    head_first(1)
    exchange(1, head_second(1, read_cotangent))
    build_forward(1, 0, 2)
    project(1, 0, 2)
    lane = lax.broadcasted_iota(jnp.int32, (ROWS, ROWS), 1)
    row = lax.broadcasted_iota(jnp.int32, (ROWS, ROWS), 0)
    perm[...] = jnp.where(lane == ((row & 63) << 3) + (row >> 6), 1.0, 0.0).astype(BF16)
    sent(0)
    exchange(2, pair_fill(1, 0, 2))
    gate_block(1, read_cotangent)
    head_params(1)
    build_backward(1)
    build_forward(0, 0, 5)
    norm_input(0)
    project(0, 0, 5)
    all_quads(pair_fill(0, 1, 5))
    sent(1)
    exchange(5, None)

    arrived(0)
    arrived(1)
    load(0, 1)
    load(1, 2)
    multiply(work, mats.at[1], mats.at[2], True)
    exchange(3, grad_fill(3))
    arrived(2)
    load(2, 0)
    multiply(work, mats.at[0], mats.at[2])
    sent(2)
    exchange(4, grad_fill(4))
    all_quads(pair_fill(0, 0, 7))
    exchange(7, None)
    out_gate(0)
    build_output(0)
    head_first(0)
    build_backward(0)
    sent(5)
    sent(3)

    arrived(3)
    tail_first(1)
    early_params(1)
    arrived(4)
    one, two = tail_second(1)

    def keep(quad):
        for k in range(4):
            c = 4 * quad + k
            rows, value = tail_value(1, c, one, two)
            upstream[rows, :] = cotangent[c].astype(F32) + value

    all_quads(keep)
    sent(4)
    exchange(6, head_second(0, read_upstream))
    late_params(1)
    sums_one(1)
    arrived(5)
    arrived(7)
    load(5, 1)
    load(7, 0)
    arrived(6)
    load(6, 2)
    multiply(work, mats.at[2], mats.at[1])
    sent(7)
    exchange(8, grad_fill(8))
    work[...] = product(mats[2], mats[0], ((0,), (0,)))
    sent(6)
    exchange(9, grad_fill(9))
    sums_two(1)
    gate_block(0, read_upstream)
    head_params(0)
    arrived(8)
    tail_first(0)
    early_params(0)
    sums_three(1)
    arrived(9)
    one, two = tail_second(0)
    late_params(0)
    sums_one(0)

    for part in range(4):
        def spread(step, carry):
            for k in range(4):
                c = part * 16 + 4 * step + k
                rows, value = tail_value(0, c, one, two)
                value = upstream[rows, :] + value
                for t in range(4):
                    block = value[:, t * 128 : (t + 1) * 128]
                    result[t, c] = block
                    send_r[t, c] = block.astype(BF16)
            return carry

        lax.fori_loop(0, 4, spread, 0)
        chans = pl.ds(part * 16, 16)
        for hi in range(2):
            pltpu.make_async_remote_copy(
                src_ref=send_r.at[2 * hi + (1 - core), chans], dst_ref=recv_r.at[part, hi],
                send_sem=send_sem.at[10 + part], recv_sem=recv_sem.at[10 + part],
                device_id={"tmpl": board * 2 + (1 - core), "row": me}, device_id_type=MESH,
            ).start()
    sums_two(0)
    for part in range(4):
        chans = pl.ds(part * 16, 16)
        wait_recv(recv_r.at[part], 10 + part, 2)
        total = result[2 * (1 - board) + core, chans] + recv_r[part, 1 - board].astype(F32)
        send_h[part] = total.astype(BF16)
        pltpu.make_async_remote_copy(
            src_ref=send_h.at[part], dst_ref=recv_h.at[part],
            send_sem=send_sem.at[14 + part], recv_sem=recv_sem.at[14 + part],
            device_id={"tmpl": (1 - board) * 2 + core, "row": me}, device_id_type=MESH,
        ).start()
    sums_three(0)
    for part in range(4):
        chans = pl.ds(part * 16, 16)
        view = recv_h.at[part]
        pltpu.make_async_copy(view, view, recv_sem.at[14 + part]).wait()
        total = result[tm, chans] + recv_r[part, board].astype(F32) + recv_h[part].astype(F32)
        trunk[chans] = total.astype(BF16)
    for d in range(2):
        wait_recv(totals.at[d], 20 + 3 * d, HALF - 1)
    for kind in (8, 9):
        sent(kind)
    for part in range(4):
        wait_send(recv_r.at[part], 10 + part, 2)
        view = recv_h.at[part]
        pltpu.make_async_copy(view, view, send_sem.at[14 + part]).wait()
    for d in range(2):
        wait_send(recv_one.at[d], 18 + 3 * d, HALF - 1)
        wait_send(recv_two.at[d], 19 + 3 * d, HALF - 1)
        wait_send(totals.at[d], 20 + 3 * d, HALF - 1)


def unpack(trunk, totals, out, grad_in, grad_out, grad_gain, grad_shift):
    out[...] = trunk[...]
    for d in range(2):
        for block in range(8):
            rows = slice(block * 8, block * 8 + 8)
            left, right = totals[d, 2 * block], totals[d, 2 * block + 1]
            grad_in[d, rows, 0:128] = left[0]
            grad_in[d, rows, 128:256] = left[1]
            grad_in[d, rows, 256:320] = right[0, :, 0:64]
            grad_out[d, rows, :] = right[0, :, 64:128]
        small = [totals[d, 2 * block + 1, 1] for block in range(8)]
        small = jnp.concatenate(small + [jnp.zeros((CH, 128), F32)], 0).T
        grad_gain[d] = small[0:2, 0:CH]
        grad_shift[d] = small[2:4, 0:CH]


def shards(saved_out, sum_out, saved_in, sum_in, cotangent, w_in, w_out, norm_gain, norm_shift):
    vmem = pl.BlockSpec(memory_space=pltpu.VMEM)
    smem = pl.BlockSpec(memory_space=pltpu.SMEM)
    shape = jax.ShapeDtypeStruct
    full = (ROWS, COLS)
    boxes = (10, PEERS, RB, COLS)
    trunk, totals = pl.pallas_call(
        kernel,
        out_shape=(shape((CH, RB, 128), BF16), shape((2, HALF, 2, 8, 128), F32)),
        in_specs=[vmem] * 7 + [smem] * 2,
        out_specs=(vmem, vmem),
        scratch_shapes=[
            pltpu.VMEM((5 * ROWS, COLS), BF16),
            pltpu.VMEM((10 * ROWS, COLS), BF16),
            pltpu.VMEM(full, BF16),
            pltpu.VMEM(full, BF16),
            pltpu.VMEM(full, BF16),
            pltpu.VMEM((2, ROWS, COLS), BF16),
            pltpu.VMEM(full, BF16),
            pltpu.VMEM(full, BF16),
            pltpu.VMEM((2, 5, ROWS, COLS), F32),
            pltpu.VMEM((4, 2, RB, COLS), F32),
            pltpu.VMEM(full, F32),
            pltpu.VMEM(full, F32),
            pltpu.VMEM(full, F32),
            pltpu.VMEM(full, F32),
            pltpu.VMEM((5 * ROWS, COLS), BF16),
            pltpu.VMEM((3, ROWS, COLS), BF16),
            pltpu.VMEM((4, CH, RB, 128), F32),
            pltpu.VMEM((CH, RB * COLS), BF16),
            pltpu.VMEM((CH, RB * COLS), BF16),
            pltpu.VMEM((3 * CH, RB * COLS), BF16),
            pltpu.VMEM((CH, 128), F32),
            pltpu.VMEM(boxes, BF16),
            pltpu.VMEM(boxes, BF16),
            pltpu.VMEM((4, CH, RB, 128), F32),
            pltpu.VMEM((4, CH, RB, 128), BF16),
            pltpu.VMEM((4, 2, 16, RB, 128), BF16),
            pltpu.VMEM((4, 16, RB, 128), BF16),
            pltpu.VMEM((4, 16, RB, 128), BF16),
            pltpu.VMEM((2, HALF, 2, 8, 128), F32),
            pltpu.VMEM((2, HALF, 2, 8, 128), F32),
            pltpu.VMEM((2, 2, 2, 8, 128), F32),
            pltpu.VMEM((2, HALF, 2, 8, 128), F32),
            pltpu.SemaphoreType.DMA((24,)),
            pltpu.SemaphoreType.DMA((24,)),
        ],
        compiler_params=pltpu.CompilerParams(
            collective_id=0, has_side_effects=True, vmem_limit_bytes=58 * 1024 * 1024
        ),
        name="triangle_backward",
    )(
        saved_out[0], sum_out[0], saved_in[0], sum_in[0], cotangent[0], w_in, w_out,
        norm_gain.reshape(4, CH), norm_shift.reshape(4, CH),
    )
    return pl.pallas_call(
        unpack,
        out_shape=(
            shape((CH, RB, 128), BF16), shape((2, CH, 5 * CH), F32), shape((2, CH, CH), F32),
            shape((2, 2, CH), F32), shape((2, 2, CH), F32),
        ),
        in_specs=[vmem] * 2,
        out_specs=(vmem,) * 5,
        name="unpack",
    )(trunk, totals)


def solution(mesh):
    whole = P("tmpl", None, "row", None)
    in_specs = (whole, whole, whole, whole, whole, P(), P(), P(), P())
    out_specs = (P(None, "row", "tmpl"), P(), P(), P(), P())
    return jax.shard_map(shards, mesh=mesh, in_specs=in_specs, out_specs=out_specs, check_vma=False)
```

```python
import functools

import jax
import jax.numpy as jnp
from jax import lax
from jax.experimental import pallas as pl
from jax.experimental.pallas import tpu as pltpu
from jax.sharding import PartitionSpec as P

EPSILON = 1e-05
F32 = jnp.float32
BF16 = jnp.bfloat16
MESH = pl.DeviceIdType.MESH
CH = 64
RB = 8
COLS = 512
ROWS = 512
PEERS = 64
HALF = 16


def sigmoid(values):
    return 0.5 * jnp.tanh(0.5 * values) + 0.5


def product(left, right, dims=((1,), (0,))):
    return lax.dot_general(left, right, (dims, ((), ())), preferred_element_type=F32)


def kernel(
    saved_out, sum_out, saved_in, sum_in, cotangent, w_in, w_out, gain, shift,
    trunk, totals,
    weights_p, weights_q, weights_u, weights_d, perm,
    normed, normed_sum, gated, proj, stat, work, update, upstream, grad_n, d_proj, mats, partial,
    lanes_n, lanes_s, lanes_r, small,
    outbox, inbox, result, send_r, recv_r, send_h, recv_h,
    param, recv_one, part_sum, recv_two,
    send_sem, recv_sem,
):
    tm = lax.axis_index("tmpl")
    me = lax.axis_index("row")
    deep, flat = me // 8, me % 8
    board, core = tm // 2, tm % 2
    saved = (saved_out, saved_in)
    sums = (sum_out, sum_in)

    barrier = pltpu.get_barrier_semaphore()

    def greet(tmpl, row):
        pl.semaphore_signal(
            barrier, inc=1, device_id={"tmpl": tmpl, "row": row}, device_id_type=MESH
        )

    def greet_row(step, carry):
        greet(tm, me ^ step)
        return carry

    lax.fori_loop(1, PEERS, greet_row, 0)

    def greet_rest(step, carry):
        greet(tm ^ 1, (deep ^ step) * 8 + flat)
        greet(tm ^ 2, deep * 8 + (flat ^ step))
        return carry

    lax.fori_loop(0, 8, greet_rest, 0)

    def rows_of(quad):
        return pl.ds(pl.multiple_of(32 * quad, 32), 32)

    def block_rows(block, quad):
        return pl.ds(pl.multiple_of(block * ROWS + 32 * quad, 32), 32)

    def to_rows(values):
        return values.astype(F32).reshape(4 * RB, COLS)

    def to_chans(values):
        return values.reshape(4, RB, COLS).astype(BF16)

    def expand_rows(table, dest, top, start):
        lane = lax.broadcasted_iota(jnp.int32, (RB, COLS), 1)
        row = lax.broadcasted_iota(jnp.int32, (RB, COLS), 0)
        mask = jnp.where((lane & 7) == row, 1.0, 0.0).astype(F32)
        work[0:CH, :] = table

        def body(step, carry):
            block = work[pl.ds(pl.multiple_of(8 * step, 8), 8), :]
            parts = [block[k : k + 1, :] * mask for k in range(8)]
            at = pl.multiple_of(top + 64 * step, 64)
            dest[pl.ds(at, 64), start : start + COLS] = jnp.concatenate(parts, 0).astype(BF16)
            return carry

        lax.fori_loop(0, CH // 8, body, 0)

    def one_hot():
        lane = lax.broadcasted_iota(jnp.int32, (CH, COLS), 1)
        row = lax.broadcasted_iota(jnp.int32, (CH, COLS), 0)
        return jnp.where((lane >> 3) == row, 1.0, 0.0).astype(BF16)

    def build_forward(d, blocks):
        spread = one_hot()
        for b in blocks:
            table = product(w_in[d, :, b * CH : (b + 1) * CH], spread, ((0,), (0,)))
            expand_rows(table, weights_p, b * ROWS, 0)

    def build_backward(d):
        spread = one_hot()
        for b in range(5):
            table = product(w_in[d, :, b * CH : (b + 1) * CH], spread)
            expand_rows(table, weights_q, 0, b * COLS)

    def build_output(d):
        spread = one_hot()
        expand_rows(product(w_out[d], spread, ((0,), (0,))), weights_u, 0, 0)
        expand_rows(product(w_out[d], spread), weights_d, 0, 0)

    def statistics(x_ref, slot):
        zero = jnp.zeros((RB, COLS), F32)

        def add(step, acc):
            for k in range(8):
                acc = acc + x_ref[8 * step + k].astype(F32)
            return acc

        mean = lax.fori_loop(0, CH // 8, add, zero) * (1.0 / CH)

        def square(step, acc):
            for k in range(8):
                off = x_ref[8 * step + k].astype(F32) - mean
                acc = acc + off * off
            return acc

        inv = lax.rsqrt(lax.fori_loop(0, CH // 8, square, zero) * (1.0 / CH) + EPSILON)
        stat[slot, 0] = mean
        stat[slot, 1] = inv
        return mean, inv

    def normalise(x_ref, mean, inv, slot, dest):
        def body(quad, carry):
            parts = []
            for k in range(4):
                c = 4 * quad + k
                standard = (x_ref[c].astype(F32) - mean) * inv
                parts.append(standard * gain[slot, c] + shift[slot, c])
            dest[rows_of(quad), :] = jnp.concatenate(parts, 0).astype(BF16)
            return carry

        lax.fori_loop(0, CH // 4, body, 0)

    def post(kind, peer):
        pltpu.make_async_remote_copy(
            src_ref=outbox.at[kind, peer], dst_ref=inbox.at[kind, me],
            send_sem=send_sem.at[kind], recv_sem=recv_sem.at[kind],
            device_id={"tmpl": tm, "row": peer}, device_id_type=MESH,
        ).start()

    def exchange(kind, fill):
        own = me // 4
        if fill is not None:
            fill(own)
        for k in range(1, 4):
            post(kind, me ^ k)

        def body(step, carry):
            quad = own ^ step
            if fill is not None:
                fill(quad)
            for k in range(4):
                post(kind, 4 * quad + k)
            return carry

        lax.fori_loop(1, PEERS // 4, body, 0)
        inbox[kind, me] = outbox[kind, me]

    def all_quads(fill):
        def body(quad, carry):
            fill(quad)
            return carry

        lax.fori_loop(0, PEERS // 4, body, 0)

    def wait_recv(dest, sem, count):
        view = dest.at[pl.ds(0, count)]
        pltpu.make_async_copy(view, view, recv_sem.at[sem]).wait()

    def wait_send(dest, sem, count):
        view = dest.at[pl.ds(0, count)]
        pltpu.make_async_copy(view, view, send_sem.at[sem]).wait()

    def arrived(kind):
        wait_recv(inbox.at[kind], kind, PEERS - 1)

    def sent(kind):
        wait_send(inbox.at[kind], kind, PEERS - 1)

    def project(d, blocks):
        for b in blocks:
            proj[d, b] = product(weights_p[b * ROWS : (b + 1) * ROWS, :], normed[d])

    def norm_input(d):
        mean, inv = statistics(saved[d], 2 * d)
        normalise(saved[d], mean, inv, 2 * d, normed.at[d])

    def pair_fill(d, k, kind):
        def fill(quad):
            rows = rows_of(quad)
            gate = sigmoid(proj[d, 2 * k, rows, :])
            proj[d, 2 * k, rows, :] = gate
            outbox[kind, pl.ds(4 * quad, 4)] = to_chans(gate * proj[d, 2 * k + 1, rows, :])

        return fill

    def out_gate(d):
        def fill(quad):
            rows = rows_of(quad)
            proj[d, 4, rows, :] = sigmoid(proj[d, 4, rows, :])

        all_quads(fill)

    def head_first(d):
        mean, inv = statistics(sums[d], 2 * d + 1)
        normalise(sums[d], mean, inv, 2 * d + 1, normed_sum)
        update[...] = product(weights_u[...], normed_sum[...])

    def backward_sums(source, x_ref, mean, inv, slot):
        keep_at = 2 * (slot % 2)

        zero = jnp.zeros((RB, COLS), F32)

        def fold(v):
            return v[:, 0:128] + v[:, 128:256] + v[:, 256:384] + v[:, 384:512]

        def body(step, carry):
            one, two = carry
            for k in range(4):
                c = 4 * step + k
                dn = source[pl.ds(pl.multiple_of(8 * c, 8), 8), :]
                standard = (x_ref[c].astype(F32) - mean) * inv
                scaled = dn * gain[slot, c]
                one = one + scaled
                two = two + scaled * standard
                partial[keep_at, c] = fold(dn * standard)
                partial[keep_at + 1, c] = fold(dn)
            return one, two

        one, two = lax.fori_loop(0, CH // 4, body, (zero, zero))
        return one * (1.0 / CH), two * (1.0 / CH)

    def small_sums(k):
        lane = lax.broadcasted_iota(jnp.int32, (CH, 128), 1)
        total = jnp.zeros((CH, 128), F32)
        for j in range(2):
            column = jnp.sum(jnp.sum(partial[2 * k + j], axis=1), axis=1, keepdims=True)
            total = total + jnp.where(lane == 2 * j + k, column, 0.0)
        return total

    def store_params(d, late, start, value, width):
        half, lane = start // 128, start % 128
        for block in range(8):
            param[d, block * 2 + half, late, :, lane : lane + width] = (
                value[block * 8 : block * 8 + 8, :]
            )

    def head_second(d, read_up):
        def gating(quad):
            rows = rows_of(quad)
            gated[rows, :] = (proj[d, 4, rows, :] * read_up(quad)).astype(BF16)

        all_quads(gating)
        work[...] = product(weights_d[...], gated[...])
        slot = 2 * d + 1
        mean, inv = stat[slot, 0], stat[slot, 1]
        one, two = backward_sums(work, sums[d], mean, inv, slot)

        def fill(quad):
            for k in range(4):
                c = 4 * quad + k
                dn = work[pl.ds(pl.multiple_of(8 * c, 8), 8), :]
                standard = (sums[d][c].astype(F32) - mean) * inv
                outbox[6 if d == 0 else 1, c] = (
                    inv * (dn * gain[slot, c] - one - standard * two)
                ).astype(BF16)

        return fill

    def gate_block(d, read_up):
        def body(quad):
            rows = rows_of(quad)
            gate = proj[d, 4, rows, :]
            d_gate = read_up(quad) * update[rows, :]
            d_proj[block_rows(4, quad), :] = (d_gate * gate * (1.0 - gate)).astype(BF16)

        all_quads(body)

    def spread_lanes(source, dest, start):
        moved = product(perm[...], source).astype(BF16)
        for r in range(RB):
            dest[start : start + CH, r * COLS : (r + 1) * COLS] = moved[r * CH : (r + 1) * CH, :]

    def head_params(d):
        spread_lanes(normed_sum[...], lanes_s, 0)
        spread_lanes(gated[...], lanes_r, 0)
        store_params(d, 0, 192, product(lanes_s[...], lanes_r[0:CH, :], ((1,), (1,))), CH)
        small[...] = small_sums(1)

    def tail_blocks(d, k):
        kind = (8 if d == 0 else 3) + k

        def body(quad):
            rows = rows_of(quad)
            grad = to_rows(inbox[kind, pl.ds(4 * quad, 4)])
            gate = proj[d, 2 * k, rows, :]
            value = proj[d, 2 * k + 1, rows, :]
            d_proj[block_rows(2 * k, quad), :] = (grad * value * gate * (1.0 - gate)).astype(BF16)
            d_proj[block_rows(2 * k + 1, quad), :] = (grad * gate).astype(BF16)

        all_quads(body)

    def tail_first(d):
        tail_blocks(d, 0)
        grad_n[...] = product(weights_q[:, 0:1024], d_proj[0:1024, :]) + product(
            weights_q[:, 2048:2560], d_proj[2048:2560, :]
        )

    def tail_second(d):
        tail_blocks(d, 1)
        grad_n[...] += product(weights_q[:, 1024:2048], d_proj[1024:2048, :])
        slot = 2 * d
        return backward_sums(grad_n, saved[d], stat[slot, 0], stat[slot, 1], slot)

    def tail_value(d, c, one, two):
        slot = 2 * d
        mean, inv = stat[slot, 0], stat[slot, 1]
        rows = pl.ds(pl.multiple_of(8 * c, 8), 8)
        standard = (saved[d][c].astype(F32) - mean) * inv
        return rows, inv * (grad_n[rows, :] * gain[slot, c] - one - standard * two)

    def early_params(d):
        spread_lanes(normed[d], lanes_n, 0)
        for at, b in enumerate((0, 1, 4)):
            spread_lanes(d_proj[b * ROWS : (b + 1) * ROWS, :], lanes_r, at * CH)
        value = product(lanes_n[...], lanes_r[0 : 3 * CH, :], ((1,), (1,)))
        store_params(d, 0, 0, value[:, 0:128], 128)
        store_params(d, 0, 128, value[:, 128:192], CH)

    def late_params(d):
        for at, b in enumerate((2, 3)):
            spread_lanes(d_proj[b * ROWS : (b + 1) * ROWS, :], lanes_r, at * CH)
        value = product(lanes_n[...], lanes_r[0 : 2 * CH, :], ((1,), (1,)))
        store_params(d, 1, 0, value, 128)
        store_params(d, 1, 128, small[...] + small_sums(0), 128)

    first = deep * 2 + core
    second = board * 8 + flat

    def to_first(d, member, source, dest, sem):
        pltpu.make_async_remote_copy(
            src_ref=source, dst_ref=dest,
            send_sem=send_sem.at[sem], recv_sem=recv_sem.at[sem],
            device_id={"tmpl": board * 2 + member % 2, "row": (member // 2) * 8 + flat},
            device_id_type=MESH,
        ).start()

    def sum_all(ref):
        total = ref[0]
        for k in range(1, HALF):
            total = total + ref[k]
        return total

    def sums_one(d):
        sem = 18 + 3 * d

        def body(step, carry):
            member = first ^ step
            to_first(d, member, param.at[d, member], recv_one.at[d, first], sem)
            return carry

        lax.fori_loop(1, HALF, body, 0)
        recv_one[d, first] = param[d, first]

    def sums_two(d):
        sem = 18 + 3 * d
        wait_recv(recv_one.at[d], sem, HALF - 1)
        part_sum[d, 0] = sum_all(recv_one.at[d])

        def body(step, carry):
            member = second ^ step
            pltpu.make_async_remote_copy(
                src_ref=part_sum.at[d, 0], dst_ref=recv_two.at[d, second],
                send_sem=send_sem.at[sem + 1], recv_sem=recv_sem.at[sem + 1],
                device_id={"tmpl": (member // 8) * 2 + core, "row": deep * 8 + member % 8},
                device_id_type=MESH,
            ).start()
            return carry

        lax.fori_loop(1, HALF, body, 0)
        recv_two[d, second] = part_sum[d, 0]

    def sums_three(d):
        sem = 18 + 3 * d
        wait_recv(recv_two.at[d], sem + 1, HALF - 1)
        part_sum[d, 1] = sum_all(recv_two.at[d]) * (1.0 / 2048.0)

        def body(step, carry):
            to_first(d, first ^ step, part_sum.at[d, 1], totals.at[d, first], sem + 2)
            return carry

        lax.fori_loop(1, HALF, body, 0)
        totals[d, first] = part_sum[d, 1]

    def load(kind, k):
        def body(quad):
            mats[k, rows_of(quad), :] = to_rows(inbox[kind, pl.ds(4 * quad, 4)]).astype(BF16)

        all_quads(body)

    def grad_fill(kind):
        def fill(quad):
            outbox[kind, pl.ds(4 * quad, 4)] = to_chans(work[rows_of(quad), :])

        return fill

    def read_cotangent(quad):
        return to_rows(cotangent[pl.ds(4 * quad, 4)])

    def read_upstream(quad):
        return upstream[rows_of(quad), :]

    build_forward(1, (2, 3))
    norm_input(1)
    project(1, (2, 3))
    pl.semaphore_wait(barrier, PEERS - 1 + 16)
    exchange(0, pair_fill(1, 1, 0))
    build_forward(1, (4,))
    build_output(1)
    project(1, (4,))
    out_gate(1)
    head_first(1)
    exchange(1, head_second(1, read_cotangent))
    build_forward(1, (0, 1))
    project(1, (0, 1))
    lane = lax.broadcasted_iota(jnp.int32, (ROWS, ROWS), 1)
    row = lax.broadcasted_iota(jnp.int32, (ROWS, ROWS), 0)
    perm[...] = jnp.where(lane == ((row & 63) << 3) + (row >> 6), 1.0, 0.0).astype(BF16)
    sent(0)
    exchange(2, pair_fill(1, 0, 2))
    gate_block(1, read_cotangent)
    head_params(1)
    build_backward(1)
    build_forward(0, (0, 1, 2, 3, 4))
    norm_input(0)

    arrived(0)
    arrived(1)
    load(0, 1)
    load(1, 2)
    work[...] = product(mats[1], mats[2], ((1,), (1,)))
    sent(1)
    exchange(3, grad_fill(3))
    project(0, (2, 3))
    arrived(2)
    load(2, 0)
    work[...] = product(mats[0], mats[2])
    sent(2)
    exchange(4, grad_fill(4))
    all_quads(pair_fill(0, 1, 5))
    project(0, (0, 1, 4))
    all_quads(pair_fill(0, 0, 7))
    out_gate(0)
    build_output(0)
    head_first(0)
    sent(3)
    exchange(5, None)

    arrived(3)
    tail_first(1)
    early_params(1)
    arrived(4)
    one, two = tail_second(1)

    def keep(quad):
        for k in range(4):
            c = 4 * quad + k
            rows, value = tail_value(1, c, one, two)
            upstream[rows, :] = cotangent[c].astype(F32) + value

    all_quads(keep)
    sent(4)
    exchange(6, head_second(0, read_upstream))
    exchange(7, None)
    gate_block(0, read_upstream)
    build_backward(0)
    sent(5)

    arrived(5)
    arrived(6)
    load(5, 1)
    load(6, 2)
    work[...] = product(mats[2], mats[1])
    sent(6)
    exchange(8, grad_fill(8))
    arrived(7)
    load(7, 0)
    work[...] = product(mats[2], mats[0], ((0,), (0,)))
    sent(7)
    exchange(9, grad_fill(9))
    late_params(1)
    sums_one(1)
    head_params(0)
    arrived(8)
    tail_first(0)
    early_params(0)
    sums_two(1)
    arrived(9)
    one, two = tail_second(0)
    late_params(0)
    sums_one(0)
    sums_three(1)

    for part in range(4):
        def spread(step, carry):
            for k in range(4):
                c = part * 16 + 4 * step + k
                rows, value = tail_value(0, c, one, two)
                value = upstream[rows, :] + value
                for t in range(4):
                    block = value[:, t * 128 : (t + 1) * 128]
                    result[t, c] = block
                    send_r[t, c] = block.astype(BF16)
            return carry

        lax.fori_loop(0, 4, spread, 0)
        chans = pl.ds(part * 16, 16)
        for hi in range(2):
            pltpu.make_async_remote_copy(
                src_ref=send_r.at[2 * hi + (1 - core), chans], dst_ref=recv_r.at[part, hi],
                send_sem=send_sem.at[10 + part], recv_sem=recv_sem.at[10 + part],
                device_id={"tmpl": board * 2 + (1 - core), "row": me}, device_id_type=MESH,
            ).start()
    sums_two(0)
    for part in range(4):
        chans = pl.ds(part * 16, 16)
        wait_recv(recv_r.at[part], 10 + part, 2)
        total = result[2 * (1 - board) + core, chans] + recv_r[part, 1 - board].astype(F32)
        send_h[part] = total.astype(BF16)
        pltpu.make_async_remote_copy(
            src_ref=send_h.at[part], dst_ref=recv_h.at[part],
            send_sem=send_sem.at[14 + part], recv_sem=recv_sem.at[14 + part],
            device_id={"tmpl": (1 - board) * 2 + core, "row": me}, device_id_type=MESH,
        ).start()
    sums_three(0)
    for part in range(4):
        chans = pl.ds(part * 16, 16)
        view = recv_h.at[part]
        pltpu.make_async_copy(view, view, recv_sem.at[14 + part]).wait()
        total = result[tm, chans] + recv_r[part, board].astype(F32) + recv_h[part].astype(F32)
        trunk[chans] = total.astype(BF16)
    for d in range(2):
        wait_recv(totals.at[d], 20 + 3 * d, HALF - 1)
    for kind in (8, 9):
        sent(kind)
    for part in range(4):
        wait_send(recv_r.at[part], 10 + part, 2)
        view = recv_h.at[part]
        pltpu.make_async_copy(view, view, send_sem.at[14 + part]).wait()
    for d in range(2):
        wait_send(recv_one.at[d], 18 + 3 * d, HALF - 1)
        wait_send(recv_two.at[d], 19 + 3 * d, HALF - 1)
        wait_send(totals.at[d], 20 + 3 * d, HALF - 1)


def unpack(trunk, totals, out, grad_in, grad_out, grad_gain, grad_shift):
    out[...] = trunk[...]
    for d in range(2):
        for block in range(8):
            rows = slice(block * 8, block * 8 + 8)
            left, right = totals[d, 2 * block], totals[d, 2 * block + 1]
            grad_in[d, rows, 0:128] = left[0]
            grad_in[d, rows, 128:256] = left[1]
            grad_in[d, rows, 256:320] = right[0, :, 0:64]
            grad_out[d, rows, :] = right[0, :, 64:128]
        small = [totals[d, 2 * block + 1, 1] for block in range(8)]
        small = jnp.concatenate(small + [jnp.zeros((CH, 128), F32)], 0).T
        grad_gain[d] = small[0:2, 0:CH]
        grad_shift[d] = small[2:4, 0:CH]


def shards(saved_out, sum_out, saved_in, sum_in, cotangent, w_in, w_out, norm_gain, norm_shift):
    vmem = pl.BlockSpec(memory_space=pltpu.VMEM)
    smem = pl.BlockSpec(memory_space=pltpu.SMEM)
    shape = jax.ShapeDtypeStruct
    full = (ROWS, COLS)
    boxes = (10, PEERS, RB, COLS)
    trunk, totals = pl.pallas_call(
        kernel,
        out_shape=(shape((CH, RB, 128), BF16), shape((2, HALF, 2, 8, 128), F32)),
        in_specs=[vmem] * 7 + [smem] * 2,
        out_specs=(vmem, vmem),
        scratch_shapes=[
            pltpu.VMEM((5 * ROWS, COLS), BF16),
            pltpu.VMEM((ROWS, 5 * COLS), BF16),
            pltpu.VMEM(full, BF16),
            pltpu.VMEM(full, BF16),
            pltpu.VMEM(full, BF16),
            pltpu.VMEM((2, ROWS, COLS), BF16),
            pltpu.VMEM(full, BF16),
            pltpu.VMEM(full, BF16),
            pltpu.VMEM((2, 5, ROWS, COLS), F32),
            pltpu.VMEM((4, 2, RB, COLS), F32),
            pltpu.VMEM(full, F32),
            pltpu.VMEM(full, F32),
            pltpu.VMEM(full, F32),
            pltpu.VMEM(full, F32),
            pltpu.VMEM((5 * ROWS, COLS), BF16),
            pltpu.VMEM((3, ROWS, COLS), BF16),
            pltpu.VMEM((4, CH, RB, 128), F32),
            pltpu.VMEM((CH, RB * COLS), BF16),
            pltpu.VMEM((CH, RB * COLS), BF16),
            pltpu.VMEM((3 * CH, RB * COLS), BF16),
            pltpu.VMEM((CH, 128), F32),
            pltpu.VMEM(boxes, BF16),
            pltpu.VMEM(boxes, BF16),
            pltpu.VMEM((4, CH, RB, 128), F32),
            pltpu.VMEM((4, CH, RB, 128), BF16),
            pltpu.VMEM((4, 2, 16, RB, 128), BF16),
            pltpu.VMEM((4, 16, RB, 128), BF16),
            pltpu.VMEM((4, 16, RB, 128), BF16),
            pltpu.VMEM((2, HALF, 2, 8, 128), F32),
            pltpu.VMEM((2, HALF, 2, 8, 128), F32),
            pltpu.VMEM((2, 2, 2, 8, 128), F32),
            pltpu.VMEM((2, HALF, 2, 8, 128), F32),
            pltpu.SemaphoreType.DMA((24,)),
            pltpu.SemaphoreType.DMA((24,)),
        ],
        compiler_params=pltpu.CompilerParams(
            collective_id=0, has_side_effects=True, vmem_limit_bytes=58 * 1024 * 1024
        ),
        name="triangle_backward",
    )(
        saved_out[0], sum_out[0], saved_in[0], sum_in[0], cotangent[0], w_in, w_out,
        norm_gain.reshape(4, CH), norm_shift.reshape(4, CH),
    )
    return pl.pallas_call(
        unpack,
        out_shape=(
            shape((CH, RB, 128), BF16), shape((2, CH, 5 * CH), F32), shape((2, CH, CH), F32),
            shape((2, 2, CH), F32), shape((2, 2, CH), F32),
        ),
        in_specs=[vmem] * 2,
        out_specs=(vmem,) * 5,
        name="unpack",
    )(trunk, totals)


def solution(mesh):
    whole = P("tmpl", None, "row", None)
    in_specs = (whole, whole, whole, whole, whole, P(), P(), P(), P())
    out_specs = (P(None, "row", "tmpl"), P(), P(), P(), P())
    return jax.shard_map(shards, mesh=mesh, in_specs=in_specs, out_specs=out_specs, check_vma=False)
```
